256 devices in a mesh: dp: 16 (over z, core), mp: 16 (over x, y).
Axes of the slice: x: 4, y: 4, z: 8, core: 2. Of those that a mesh axis runs over, the one named last changes fastest.
Arguments:
- gradients: bfloat16 [64, 2, 4096, 512], P('mp', None, 'dp'), may hold values from -50 to 50
- moments: bfloat16 [64, 2, 4096, 512], P('mp', None, 'dp'), may hold values from -6 to 6
- weights: bfloat16 [64, 2, 4096, 512], P('mp', None, 'dp'), may hold values from -6 to 6
- head_logits: float32 [16, 64, 32], P('mp'), may hold values from 10 to 200
Outputs:
- new_weights: bfloat16 [64, 2, 4096, 512], P('mp', None, 'dp')
- new_moments: bfloat16 [64, 2, 4096, 512], P('mp', None, 'dp')
- updates: bfloat16 [64, 2, 4096, 512], P('mp', None, 'dp')
The draws below stay inside these ranges and needn't reach their ends.
All inputs are finite; a program needn't handle non-finite values.
Results may differ from the reference program's by a relative error of at most 0.0086.
Values may be sent and summed in bfloat16 or wider, within the bound.
No kernel may reach another device: no remote copies, remote signals or barrier semaphores. Data moves between devices by JAX's collectives and lax.ppermute only.
A program may use at most 64 MiB of HBM per device.

```python
import math
import jax
import jax.numpy as jnp
from jax import lax

H = 32
DK = 128
R = 512
ITERS = 3
NH = 4096
LAYERS = 64
N_MP = 16


def draw_gradients(key, part):
    key = jax.random.fold_in(key, 7)
    base_key, row_key, column_key = jax.random.split(key, 3)
    full_shape = (LAYERS, 2, NH, R)
    row_scale = jnp.exp(jax.random.uniform(row_key, (LAYERS, 2, NH, 1), jnp.float32, -1.15, 1.15))
    column_scale = jnp.exp(jax.random.uniform(column_key, (LAYERS, 2, 1, R), jnp.float32, -1.15, 1.15))
    base_values = jnp.clip(jax.random.normal(base_key, full_shape, jnp.float32), -5.0, 5.0)
    return (base_values * row_scale * column_scale).astype(jnp.bfloat16)


def steps_of(key, extent, cuts, low, high):
    def one(position, shards_of):
        draws = jax.random.uniform(jax.random.fold_in(jax.random.fold_in(key, 6), position), (shards_of,), jnp.float32, low / len(cuts), high / len(cuts))
        return jnp.repeat(jnp.exp(draws), extent[position] // shards_of).reshape((-1,) + (1,) * (len(extent) - position - 1))

    level = one(*cuts[0])
    for cut in cuts[1:]:
        level = level * one(*cut)
    return level


def gaussian(key, shape, width, most, cuts=(), held_as=jnp.bfloat16):
    loudness = steps_of(key, shape, cuts, -0.22, 0.18) if cuts else 1.0
    values = jax.random.normal(key, shape, jnp.float32) * width * loudness
    return jnp.minimum(jnp.maximum(values, -most), most).astype(held_as)


def setup_inputs(seed: int = 0) -> dict:
    splits = jax.random.split(jax.random.key(seed), 5)
    gradients = draw_gradients(jax.random.fold_in(splits[4], 71), 0)
    moments = gaussian(splits[1], (LAYERS, 2, NH, R), 1.0, 6.0, ((0, 16), (2, 16)))
    weights = gaussian(splits[2], (LAYERS, 2, NH, R), 1.0, 6.0, ((0, 16), (2, 16)))
    head_logits = jnp.clip(jnp.exp(math.log(200.0) - 2.9957323 * jax.random.uniform(splits[3], (N_MP, LAYERS, H), jnp.float32) ** steps_of(splits[3], (N_MP, LAYERS, H), ((0, 16),), -0.2, 0.2)), 10.0, 200.0)
    return {"gradients": gradients, "moments": moments, "weights": weights, "head_logits": head_logits}


FIRST_COEFF = 3.4445
SECOND_COEFF = -4.775
THIRD_COEFF = 2.0315
MOMENTUM = 0.95
LEARN_RATE = 0.1
SHRINK = 0.99
CLIP_LIMIT = 100.0
EPSILON = 1e-07

def orthogonal(advance):
    widened = advance.astype(jnp.float32)
    squares = jnp.sum(widened * widened)
    current = (widened / (jnp.sqrt(squares) + EPSILON)).astype(jnp.bfloat16)
    for _ in range(ITERS):
        gram_matrix = lax.dot_general(current, current, (((0,), (0,)), ((), ())), preferred_element_type=jnp.float32)
        gram_low = lax.optimization_barrier(gram_matrix.astype(jnp.bfloat16))
        square = jnp.dot(gram_low, gram_low, preferred_element_type=jnp.float32)
        polynomial = (SECOND_COEFF * gram_low.astype(jnp.float32) + THIRD_COEFF * square).astype(jnp.bfloat16)
        current = (FIRST_COEFF * current.astype(jnp.float32) + jnp.dot(current, polynomial, preferred_element_type=jnp.float32)).astype(jnp.bfloat16)
    return current

def one_matrix(items):
    gradient, moment, weight, factor = items
    widened = gradient.astype(jnp.float32)
    moment_sum = MOMENTUM * moment.astype(jnp.float32) + widened
    new_moment = moment_sum.astype(jnp.bfloat16)
    advance = (widened + MOMENTUM * moment_sum).astype(jnp.bfloat16)
    ortho_rows = orthogonal(advance)
    scaled = 0.2 * math.sqrt(max(NH, R)) * ortho_rows.astype(jnp.float32)
    update = scaled.astype(jnp.bfloat16)
    new_weight = ((weight.astype(jnp.float32) * SHRINK - LEARN_RATE * scaled) * factor).astype(jnp.bfloat16)
    return (new_weight, new_moment, update)

def reference(gradients, moments, weights, head_logits):
    peak_logit = lax.optimization_barrier(jnp.max(head_logits, axis=0))
    clip_ratio = jnp.sqrt(jnp.minimum(1.0, CLIP_LIMIT / peak_logit))
    key_factor = jnp.repeat(clip_ratio, DK, axis=1)
    factor = jnp.stack([key_factor, jnp.ones_like(key_factor)], axis=1)[..., None]
    matrix_count = LAYERS * 2
    outputs = lax.map(one_matrix, (gradients.reshape(matrix_count, NH, R), moments.reshape(matrix_count, NH, R), weights.reshape(matrix_count, NH, R), factor.reshape(matrix_count, NH, 1)))
    new_weights = outputs[0].reshape(LAYERS, 2, NH, R)
    new_moments = outputs[1].reshape(LAYERS, 2, NH, R)
    updates = outputs[2].reshape(LAYERS, 2, NH, R)
    return (new_weights, new_moments, updates)
```

```python
import math

import jax
import jax.numpy as jnp
from jax import lax
from jax.experimental import pallas as pl
from jax.experimental.pallas import tpu as pltpu
from jax.sharding import PartitionSpec as P

DK = 128
SIDE = 128
EXTRA = 32
PACKED = 8 * SIDE + EXTRA
HALF = PACKED // 2
MEBI = 1024 * 1024

FIRST_COEFF = 3.4445
SECOND_COEFF = -4.775
THIRD_COEFF = 2.0315
MOMENTUM = 0.95
LEARN_RATE = 0.1
SHRINK = 0.99
CLIP_LIMIT = 100.0
EPSILON = 1e-07


def low(value):
    return value.astype(jnp.bfloat16)


def wide(value):
    return value.astype(jnp.float32)


def product(left, right):
    return jnp.dot(low(left), low(right), preferred_element_type=jnp.float32)


def square_iota(dimension):
    return lax.broadcasted_iota(jnp.int32, (SIDE, SIDE), dimension)


def diagonal_row(block):
    return jnp.sum(jnp.where(square_iota(0) == square_iota(1), block, 0.0), axis=0, keepdims=True)


ORDER = ((0, 1), (0, 2), (0, 3)), ((1, 2), (1, 3), (2, 3))


def pack(blocks, residuals=False):
    upper = square_iota(0) <= square_iota(1)
    pieces = []
    for which in range(2):
        even, odd = blocks[2 * which, 2 * which], blocks[2 * which + 1, 2 * which + 1]
        pieces.append(jnp.where(upper, even, odd))
        pieces += [blocks[name] for name in ORDER[which]]
    row = lax.broadcasted_iota(jnp.int32, (EXTRA, SIDE), 0)
    extra = jnp.zeros((EXTRA, SIDE), jnp.float32)
    for i in range(4):
        values = diagonal_row(blocks[i, i])
        extra = jnp.where(row == i, values, extra)
        if residuals:
            extra = jnp.where(row == 4 + i, values - wide(low(values)), extra)
    return jnp.concatenate([low(piece) for piece in pieces + [extra]], axis=0)


def unpack_blocks(packed, dtype):
    rows, columns = square_iota(0), square_iota(1)
    extra = wide(packed[8 * SIDE :])
    blocks = {}
    for which in range(2):
        pieces = [packed[(4 * which + k) * SIDE : (4 * which + k + 1) * SIDE] for k in range(4)]
        both = wide(pieces[0])
        turned = both.T
        first, second = extra[2 * which : 2 * which + 1], extra[2 * which + 1 : 2 * which + 2]
        even = jnp.where(rows < columns, both, jnp.where(rows > columns, turned, first))
        odd = jnp.where(rows > columns, both, jnp.where(rows < columns, turned, second))
        blocks[2 * which, 2 * which] = even.astype(dtype)
        blocks[2 * which + 1, 2 * which + 1] = odd.astype(dtype)
        for name, piece in zip(ORDER[which], pieces[1:]):
            blocks[name] = piece.astype(dtype)
    return blocks, extra


def corner(blocks, i):
    right = blocks[i, i + 1]
    return jnp.concatenate(
        [
            jnp.concatenate([blocks[i, i], right], axis=1),
            jnp.concatenate([wide(right).T.astype(right.dtype), blocks[i + 1, i + 1]], axis=1),
        ],
        axis=0,
    )


def off_corner(blocks):
    return jnp.concatenate(
        [jnp.concatenate([blocks[i, 2], blocks[i, 3]], axis=1) for i in (0, 1)], axis=0
    )


def cut_blocks(matrix):
    return {
        (i, j): matrix[i * SIDE : (i + 1) * SIDE, j * SIDE : (j + 1) * SIDE]
        for i in range(4)
        for j in range(i, 4)
    }


def gram_kernel(
    place_ref, grad_ref, moment_ref, new_moment_ref, advance_ref,
    mine_ref, theirs_ref, far_mine_ref, far_theirs_ref, own_ref,
):
    step = pl.program_id(0)
    widened = wide(grad_ref[0])
    moment_sum = MOMENTUM * wide(moment_ref[0]) + widened
    new_moment_ref[0] = low(moment_sum)
    advance = low(widened + MOMENTUM * moment_sum)
    advance_ref[0] = advance
    middle = 2 * SIDE
    contract = (((0,), (0,)), ((), ()))
    upper = lax.dot_general(
        advance[:, :middle], advance, contract, preferred_element_type=jnp.float32
    )
    lower = lax.dot_general(
        advance[:, middle:], advance[:, middle:], contract, preferred_element_type=jnp.float32
    )
    blocks = {}
    for i in range(2):
        for j in range(i, 4):
            blocks[i, j] = upper[i * SIDE : (i + 1) * SIDE, j * SIDE : (j + 1) * SIDE]
        for j in range(i, 2):
            blocks[i + 2, j + 2] = lower[i * SIDE : (i + 1) * SIDE, j * SIDE : (j + 1) * SIDE]
    packed = pack(blocks)

    @pl.when(step == 0)
    def _():
        on_first = place_ref[1] == 0
        far_mine_ref[...] = jnp.where(on_first, packed[:HALF], packed[HALF:])
        far_theirs_ref[...] = jnp.where(on_first, packed[HALF:], packed[:HALF])

    @pl.when(jnp.logical_and(step % 2 == 1, step < 7))
    def _():
        mine_ref[0] = packed

    @pl.when(jnp.logical_and(step % 2 == 0, step > 0))
    def _():
        theirs_ref[0] = packed

    @pl.when(step == 7)
    def _():
        own_ref[...] = packed


def grams(place, gradients, moments):
    matrices, rows, width = gradients.shape

    def own(step, place):
        distance = 4 - (step + 1) // 2
        carried = (step % 2) == 1
        up = jnp.logical_xor(carried, place[1] == 1)
        signed = jnp.where(up, distance, matrices - distance)
        return (lax.rem(place[0] + signed, matrices), 0, 0)

    def slot(step, place):
        return (jnp.clip((step - 1) // 2, 0, 2), 0, 0)

    full = pl.BlockSpec((1, rows, width), own)
    packed = pl.BlockSpec((1, PACKED, SIDE), slot)
    half = pl.BlockSpec((HALF, SIDE), lambda step, place: (0, 0))
    whole = pl.BlockSpec((PACKED, SIDE), lambda step, place: (0, 0))
    full_shape = jax.ShapeDtypeStruct(gradients.shape, jnp.bfloat16)
    packed_shape = jax.ShapeDtypeStruct((3, PACKED, SIDE), jnp.bfloat16)
    half_shape = jax.ShapeDtypeStruct((HALF, SIDE), jnp.bfloat16)
    whole_shape = jax.ShapeDtypeStruct((PACKED, SIDE), jnp.bfloat16)
    return pl.pallas_call(
        gram_kernel,
        out_shape=(
            full_shape, full_shape, packed_shape, packed_shape, half_shape, half_shape, whole_shape,
        ),
        grid_spec=pltpu.PrefetchScalarGridSpec(
            num_scalar_prefetch=1,
            grid=(matrices,),
            in_specs=[full, full],
            out_specs=(full, full, packed, packed, half, half, whole),
        ),
        compiler_params=pltpu.CompilerParams(vmem_limit_bytes=60 * MEBI),
        cost_estimate=pl.CostEstimate(
            flops=2 * gradients.size * width, bytes_accessed=10 * gradients.size, transcendentals=0
        ),
    )(place, gradients, moments)


def polynomial_kernel(mine_ref, theirs_ref, peaks_ref, out_ref, ratio_ref):
    ratio_ref[...] = jnp.sqrt(jnp.minimum(1.0, CLIP_LIMIT / peaks_ref[...]))
    blocks, _ = unpack_blocks(wide(mine_ref[...]) + wide(theirs_ref[...]), jnp.float32)
    corners = off_corner(blocks)
    gram = jnp.concatenate(
        [
            jnp.concatenate([corner(blocks, 0), corners], axis=1),
            jnp.concatenate([corners.T, corner(blocks, 2)], axis=1),
        ],
        axis=0,
    )
    width = gram.shape[0]
    rows = lax.broadcasted_iota(jnp.int32, (width, width), 0)
    columns = lax.broadcasted_iota(jnp.int32, (width, width), 1)
    diagonal = rows == columns
    norm = jnp.sqrt(jnp.sum(jnp.where(diagonal, gram, 0.0)))
    scale = 1.0 / (norm + EPSILON)
    gram = gram * scale * scale

    def poly(gram):
        return SECOND_COEFF * gram + THIRD_COEFF * product(gram, gram)

    def following(gram, step):
        inner = FIRST_COEFF * gram + product(gram, step)
        return FIRST_COEFF * inner + product(inner, step)

    rest = poly(gram)
    factor = FIRST_COEFF
    gram = following(gram, rest)
    for last in (False, True):
        step = poly(gram)
        if not last:
            gram = following(gram, step)
        rest = FIRST_COEFF * rest + factor * step + product(rest, step)
        factor = factor * FIRST_COEFF
    total = jnp.where(diagonal, rest + factor, rest) * scale
    out_ref[...] = pack(cut_blocks(total), residuals=True)


def polynomial(mine, theirs, peaks):
    width = 4 * SIDE
    whole = pl.BlockSpec(memory_space=pltpu.VMEM)
    return pl.pallas_call(
        polynomial_kernel,
        out_shape=(
            jax.ShapeDtypeStruct((PACKED, SIDE), jnp.bfloat16),
            jax.ShapeDtypeStruct(peaks.shape, jnp.float32),
        ),
        in_specs=[whole, whole, whole],
        out_specs=(whole, whole),
        compiler_params=pltpu.CompilerParams(vmem_limit_bytes=40 * MEBI),
        cost_estimate=pl.CostEstimate(
            flops=9 * 2 * width**3, bytes_accessed=6 * PACKED * SIDE, transcendentals=0
        ),
    )(mine, theirs, peaks)


def finish(place, factors, advance, weights, pieces, distance, results):
    matrices, rows, width = advance.shape
    count = len(pieces)
    middle = width // 2
    scaling = 0.2 * math.sqrt(max(rows * matrices * 2, width))

    def index(step, place):
        below = jnp.logical_xor(step == 1, place[1] == 0)
        signed = jnp.where(below, matrices - distance, distance)
        return lax.rem(place[0] + signed, matrices)

    def kernel(place_ref, factor_ref, advance_ref, weight_ref, *refs):
        new_weight_ref, update_ref, place_out_ref = refs[-4:-1]
        place_out_ref[0] = place_ref[0]
        place_out_ref[1] = place_ref[1]
        matrix_ref = refs[-1]
        step = pl.program_id(0)
        for k in range(count):

            @pl.when(step == k)
            def _():
                blocks, extra = unpack_blocks(refs[k][...], jnp.bfloat16)
                matrix_ref[:middle, :middle] = corner(blocks, 0)
                matrix_ref[:middle, middle:] = off_corner(blocks)
                matrix_ref[middle:width, middle:] = corner(blocks, 2)
                for i in range(4):
                    matrix_ref[width:, i * SIDE : (i + 1) * SIDE] = low(
                        jnp.broadcast_to(extra[4 + i : 5 + i], (16, SIDE))
                    )

        which = index(step, place_ref)
        row = lax.broadcasted_iota(jnp.int32, (rows, 1), 0)
        factor = jnp.where(row < DK, factor_ref[2 * which], factor_ref[2 * which + 1])
        off = matrix_ref[:middle, middle:]
        left, right = advance_ref[0, :, :middle], advance_ref[0, :, middle:]
        halves = (
            jnp.dot(left, matrix_ref[:middle, :middle], preferred_element_type=jnp.float32)
            + lax.dot_general(
                right, off, (((1,), (1,)), ((), ())), preferred_element_type=jnp.float32
            ),
            jnp.dot(left, off, preferred_element_type=jnp.float32)
            + jnp.dot(right, matrix_ref[middle:width, middle:], preferred_element_type=jnp.float32),
        )
        for k, values in enumerate((left, right)):
            columns = slice(k * middle, (k + 1) * middle)
            rest = wide(matrix_ref[width : width + 1, columns])
            scaled = scaling * (halves[k] + wide(values) * rest)
            update_ref[0, :, columns] = low(scaled)
            new_weight = (wide(weight_ref[0, :, columns]) * SHRINK - LEARN_RATE * scaled) * factor
            new_weight_ref[0, :, columns] = low(new_weight)

    full = pl.BlockSpec((1, rows, width), lambda step, place, factors: (index(step, place), 0, 0))
    whole = pl.BlockSpec((PACKED, SIDE), lambda step, place, factors: (0, 0))
    anywhere = pl.BlockSpec(memory_space=pl.ANY)
    shape = jax.ShapeDtypeStruct(advance.shape, jnp.bfloat16)
    carried = [] if results is None else list(results)
    first_carried = 4 + count
    return pl.pallas_call(
        kernel,
        out_shape=(shape, shape, jax.ShapeDtypeStruct((2,), jnp.int32)),
        grid_spec=pltpu.PrefetchScalarGridSpec(
            num_scalar_prefetch=2,
            grid=(count,),
            in_specs=[full, full] + [whole] * count + [anywhere] * len(carried),
            out_specs=(full, full, pl.BlockSpec(memory_space=pltpu.SMEM)),
            scratch_shapes=[pltpu.VMEM((width + 16, width), jnp.bfloat16)],
        ),
        input_output_aliases={first_carried + k: k for k in range(len(carried))},
        compiler_params=pltpu.CompilerParams(vmem_limit_bytes=48 * MEBI),
        cost_estimate=pl.CostEstimate(
            flops=2 * count * rows * width * width,
            bytes_accessed=count * (8 * rows * width + 2 * PACKED * SIDE),
            transcendentals=0,
        ),
    )(place, factors, advance, weights, *pieces, *carried)


def own_peaks_of(logits, observers):
    index = lax.axis_index("mp")
    peaks = logits
    bit = observers // 2
    while bit:
        low_part, high_part = jnp.split(peaks, 2, axis=0)
        upper = (index // bit) % 2 == 1
        sent = jnp.where(upper, low_part, high_part)
        kept = jnp.where(upper, high_part, low_part)
        pairs = [(i, i ^ bit) for i in range(observers)]
        peaks = jnp.maximum(kept, lax.ppermute(sent, "mp", pairs))
        bit //= 2
    return peaks


def shards(gradients, moments, weights, head_logits):
    layers, kind_count, row_count, latent_width = gradients.shape
    matrices = layers * kind_count
    parties = lax.axis_size("dp")
    dp = lax.axis_index("dp")
    core = dp % 2
    place = jnp.stack([dp // 2, core]).astype(jnp.int32)
    stacked = (matrices, row_count, latent_width)

    swap_pairs = [(i, i ^ 1) for i in range(parties)]
    ring_pairs = [(i, (i + 2 - 4 * (i % 2)) % parties) for i in range(parties)]

    def swap(value):
        return lax.ppermute(value, "dp", swap_pairs)

    def onward(value):
        return lax.ppermute(value, "dp", ring_pairs)

    new_moments, advance, mine, theirs, far_mine, far_theirs, own = grams(
        place, gradients.reshape(stacked), moments.reshape(stacked)
    )
    far = onward(low(wide(far_mine) + wide(swap(far_theirs))))
    arrived = swap(theirs)
    blank = jnp.zeros((HALF, SIDE), jnp.float32)
    running = jnp.concatenate(
        [jnp.where(core == 0, wide(far), blank), jnp.where(core == 0, blank, wide(far))], axis=0
    )
    for slot in range(3):
        running = wide(onward(low(wide(mine[slot]) + wide(arrived[slot]) + running)))
    partial = low(wide(own) + running)
    peaks = own_peaks_of(head_logits[0], lax.axis_size("mp"))
    piece, clip_ratio = polynomial(partial, swap(partial), peaks)

    heads = row_count // DK
    key_factor = lax.dynamic_slice_in_dim(clip_ratio, dp * heads, heads, 1)
    factors = jnp.stack([key_factor, jnp.ones_like(key_factor)], axis=1).reshape(-1)

    def final(pieces, distance, results):
        *results, after = finish(
            place, factors, advance, weights.reshape(stacked), pieces, distance, results
        )
        return results, after

    results, _ = final([piece], 0, None)
    piece = onward(piece)
    results, after = final([piece, swap(piece)], 1, results)
    piece = onward(piece)
    results, later = final([piece, swap(piece)], 2, results)
    piece = onward(piece)
    results, _ = final([piece, swap(piece)], 3, results)
    last = onward(jnp.where(after[1] == 0, piece[:HALF], piece[HALF:]))
    last = jnp.where(later[1] < 0, jnp.zeros_like(last), last)
    other = swap(last)
    halves = [jnp.where(core == 0, last, other), jnp.where(core == 0, other, last)]
    (new_weights, updates), _ = final([jnp.concatenate(halves, axis=0)], 4, results)
    whole = gradients.shape
    return (new_weights.reshape(whole), new_moments.reshape(whole), updates.reshape(whole))


def solution(mesh):
    return jax.shard_map(
        shards,
        mesh=mesh,
        in_specs=(
            P("mp", None, "dp", None),
            P("mp", None, "dp", None),
            P("mp", None, "dp", None),
            P("mp", None, None),
        ),
        out_specs=(P("mp", None, "dp", None), P("mp", None, "dp", None), P("mp", None, "dp", None)),
        check_vma=False,
    )
```

```python
import math

import jax
import jax.numpy as jnp
from jax import lax
from jax.experimental import pallas as pl
from jax.experimental.pallas import tpu as pltpu
from jax.sharding import PartitionSpec as P

DK = 128
SIDE = 128
SQUARES = 8 * SIDE
GRAM_ROWS = SQUARES + 64
GRAM_HALF = GRAM_ROWS // 2
PACKED = SQUARES + 32
HALF = PACKED // 2
MEBI = 1024 * 1024

FIRST_COEFF = 3.4445
SECOND_COEFF = -4.775
THIRD_COEFF = 2.0315
MOMENTUM = 0.95
LEARN_RATE = 0.1
SHRINK = 0.99
CLIP_LIMIT = 100.0
EPSILON = 1e-07


def low(value):
    return value.astype(jnp.bfloat16)


def wide(value):
    return value.astype(jnp.float32)


def product(left, right):
    return jnp.dot(low(left), low(right), preferred_element_type=jnp.float32)


def square_iota(dimension):
    return lax.broadcasted_iota(jnp.int32, (SIDE, SIDE), dimension)


def diagonal_row(block):
    return jnp.sum(jnp.where(square_iota(0) == square_iota(1), block, 0.0), axis=0, keepdims=True)


ORDER = ((0, 1), (0, 2), (0, 3)), ((1, 2), (1, 3), (2, 3))


def pack(blocks, rows, residuals=False):
    upper = square_iota(0) <= square_iota(1)
    pieces = []
    for which in range(2):
        even, odd = blocks[2 * which, 2 * which], blocks[2 * which + 1, 2 * which + 1]
        pieces.append(jnp.where(upper, even, odd))
        pieces += [blocks[name] for name in ORDER[which]]
    row = lax.broadcasted_iota(jnp.int32, (rows - SQUARES, SIDE), 0)
    extra = jnp.zeros(row.shape, jnp.float32)
    for i in range(4):
        values = diagonal_row(blocks[i, i])
        extra = jnp.where(row == i, values, extra)
        if residuals:
            extra = jnp.where(row == 4 + i, values - wide(low(values)), extra)
    return jnp.concatenate([low(piece) for piece in pieces + [extra]], axis=0)


def unpack_blocks(packed, dtype):
    rows, columns = square_iota(0), square_iota(1)
    extra = wide(packed[SQUARES:])
    blocks = {}
    for which in range(2):
        pieces = [packed[(4 * which + k) * SIDE : (4 * which + k + 1) * SIDE] for k in range(4)]
        both = wide(pieces[0])
        turned = both.T
        first, second = extra[2 * which : 2 * which + 1], extra[2 * which + 1 : 2 * which + 2]
        even = jnp.where(rows < columns, both, jnp.where(rows > columns, turned, first))
        odd = jnp.where(rows > columns, both, jnp.where(rows < columns, turned, second))
        blocks[2 * which, 2 * which] = even.astype(dtype)
        blocks[2 * which + 1, 2 * which + 1] = odd.astype(dtype)
        for name, piece in zip(ORDER[which], pieces[1:]):
            blocks[name] = piece.astype(dtype)
    return blocks, extra


def corner(blocks, i):
    right = blocks[i, i + 1]
    return jnp.concatenate(
        [
            jnp.concatenate([blocks[i, i], right], axis=1),
            jnp.concatenate([wide(right).T.astype(right.dtype), blocks[i + 1, i + 1]], axis=1),
        ],
        axis=0,
    )


def off_corner(blocks):
    return jnp.concatenate(
        [jnp.concatenate([blocks[i, 2], blocks[i, 3]], axis=1) for i in (0, 1)], axis=0
    )


def cut_blocks(matrix):
    return {
        (i, j): matrix[i * SIDE : (i + 1) * SIDE, j * SIDE : (j + 1) * SIDE]
        for i in range(4)
        for j in range(i, 4)
    }


def carried(step):
    return 4 - (step + 1) // 2, (step % 2) == 1


def gram_kernel(
    grad_hbm, moment_hbm,
    new_moment_hbm, advance_hbm, mine_hbm, theirs_hbm, far_mine_hbm, far_theirs_hbm, own_hbm,
    grad_ref, moment_ref, new_moment_ref, advance_ref, packed_ref, in_sems, out_sems,
):
    matrices, rows, width = grad_ref.shape
    dp = lax.axis_index("dp")
    chip, core = dp // 2, dp % 2
    middle = width // 2
    contract = (((0,), (0,)), ((), ()))

    def place_of(step):
        distance, mine = carried(step)
        up = core == (0 if mine else 1)
        return lax.rem(chip + jnp.where(up, distance, matrices - distance), matrices)

    def incoming(step, which):
        source, target = ((grad_hbm, grad_ref), (moment_hbm, moment_ref))[which]
        return pltpu.make_async_copy(
            source.at[place_of(step)], target.at[step], in_sems.at[which, step]
        )

    def outgoing(step, which):
        source, target = ((new_moment_ref, new_moment_hbm), (advance_ref, advance_hbm))[which]
        return pltpu.make_async_copy(
            source.at[step], target.at[place_of(step)], out_sems.at[which, step]
        )

    def packed_copy(source, target, sem):
        return pltpu.make_async_copy(source, target, sem)

    for step in range(matrices):
        incoming(step, 0).start()
        incoming(step, 1).start()
    copies = []
    for step in range(matrices):
        incoming(step, 0).wait()
        incoming(step, 1).wait()
        widened = wide(grad_ref[step])
        moment_sum = MOMENTUM * wide(moment_ref[step]) + widened
        new_moment_ref[step] = low(moment_sum)
        advance = low(widened + MOMENTUM * moment_sum)
        advance_ref[step] = advance
        for which in range(2):
            copies.append(outgoing(step, which))
            copies[-1].start()
        upper = lax.dot_general(
            advance[:, :middle], advance, contract, preferred_element_type=jnp.float32
        )
        lower = lax.dot_general(
            advance[:, middle:], advance[:, middle:], contract, preferred_element_type=jnp.float32
        )
        blocks = {}
        for i in range(2):
            for j in range(i, 4):
                blocks[i, j] = upper[i * SIDE : (i + 1) * SIDE, j * SIDE : (j + 1) * SIDE]
            for j in range(i, 2):
                blocks[i + 2, j + 2] = lower[i * SIDE : (i + 1) * SIDE, j * SIDE : (j + 1) * SIDE]
        packed = pack(blocks, GRAM_ROWS)
        mine = step in (0, matrices - 1) or carried(step)[1]
        natural = core == (0 if mine else 1)
        packed_ref[step, :GRAM_HALF] = jnp.where(natural, packed[:GRAM_HALF], packed[GRAM_HALF:])
        packed_ref[step, GRAM_HALF:] = jnp.where(natural, packed[GRAM_HALF:], packed[:GRAM_HALF])
        if step == 0:
            first, second = packed_ref.at[0, :GRAM_HALF], packed_ref.at[0, GRAM_HALF:]
            copies.append(packed_copy(first, far_mine_hbm, out_sems.at[2, 0]))
            copies[-1].start()
            copies.append(packed_copy(second, far_theirs_hbm, out_sems.at[3, 0]))
            copies[-1].start()
            continue
        if step == matrices - 1:
            target = own_hbm
        elif mine:
            target = mine_hbm.at[(step - 1) // 2]
        else:
            target = theirs_hbm.at[(step - 1) // 2]
        copies.append(packed_copy(packed_ref.at[step], target, out_sems.at[2, step]))
        copies[-1].start()
    for copy in copies:
        copy.wait()


def grams(gradients, moments):
    matrices, rows, width = gradients.shape
    there = pl.BlockSpec(memory_space=pltpu.HBM)
    anywhere = pl.BlockSpec(memory_space=pl.ANY)

    def shape(*sizes):
        return jax.ShapeDtypeStruct(sizes, jnp.bfloat16)

    full = shape(*gradients.shape)
    return pl.pallas_call(
        gram_kernel,
        out_shape=(
            full, full, shape(3, GRAM_ROWS, SIDE), shape(3, GRAM_ROWS, SIDE),
            shape(GRAM_HALF, SIDE), shape(GRAM_HALF, SIDE), shape(GRAM_ROWS, SIDE),
        ),
        in_specs=[there, there],
        out_specs=(there, there) + (anywhere,) * 5,
        scratch_shapes=[pltpu.VMEM(gradients.shape, jnp.bfloat16)] * 4
        + [
            pltpu.VMEM((matrices, GRAM_ROWS, SIDE), jnp.bfloat16),
            pltpu.SemaphoreType.DMA((2, matrices)),
            pltpu.SemaphoreType.DMA((4, matrices)),
        ],
        compiler_params=pltpu.CompilerParams(vmem_limit_bytes=50 * MEBI),
        cost_estimate=pl.CostEstimate(
            flops=2 * gradients.size * width, bytes_accessed=10 * gradients.size, transcendentals=0
        ),
    )(gradients, moments)


def polynomial_kernel(place_ref, mine_ref, theirs_ref, first_ref, second_ref, ratio_ref):
    natural = place_ref[1] == 0
    mine, theirs = wide(mine_ref[...]), wide(theirs_ref[...])
    first = mine[:GRAM_HALF] + theirs[GRAM_HALF:]
    second = mine[GRAM_HALF:] + theirs[:GRAM_HALF]
    packed = jnp.concatenate(
        [jnp.where(natural, first, second), jnp.where(natural, second, first)], axis=0
    )
    blocks, extra = unpack_blocks(packed, jnp.float32)
    logits = extra[16:32] + extra[32:48] + extra[48:64]
    peaks = jnp.max(logits, axis=0, keepdims=True)
    ratio_ref[...] = jnp.sqrt(jnp.minimum(1.0, CLIP_LIMIT / peaks))
    corners = off_corner(blocks)
    gram = jnp.concatenate(
        [
            jnp.concatenate([corner(blocks, 0), corners], axis=1),
            jnp.concatenate([corners.T, corner(blocks, 2)], axis=1),
        ],
        axis=0,
    )
    width = gram.shape[0]
    rows = lax.broadcasted_iota(jnp.int32, (width, width), 0)
    columns = lax.broadcasted_iota(jnp.int32, (width, width), 1)
    diagonal = rows == columns
    norm = jnp.sqrt(jnp.sum(jnp.where(diagonal, gram, 0.0)))
    scale = 1.0 / (norm + EPSILON)
    gram = gram * scale * scale

    def poly(gram):
        return SECOND_COEFF * gram + THIRD_COEFF * product(gram, gram)

    def following(gram, step):
        inner = FIRST_COEFF * gram + product(gram, step)
        return FIRST_COEFF * inner + product(inner, step)

    rest = poly(gram)
    factor = FIRST_COEFF
    gram = following(gram, rest)
    for last in (False, True):
        step = poly(gram)
        if not last:
            gram = following(gram, step)
        rest = FIRST_COEFF * rest + factor * step + product(rest, step)
        factor = factor * FIRST_COEFF
    total = jnp.where(diagonal, rest + factor, rest) * scale
    packed = pack(cut_blocks(total), PACKED, residuals=True)
    first_ref[...] = jnp.where(natural, packed[:HALF], packed[HALF:])
    second_ref[...] = jnp.where(natural, packed[HALF:], packed[:HALF])


def polynomial(place, mine, theirs):
    width = 4 * SIDE
    whole = pl.BlockSpec(memory_space=pltpu.VMEM)
    return pl.pallas_call(
        polynomial_kernel,
        out_shape=(
            jax.ShapeDtypeStruct((HALF, SIDE), jnp.bfloat16),
            jax.ShapeDtypeStruct((HALF, SIDE), jnp.bfloat16),
            jax.ShapeDtypeStruct((1, SIDE), jnp.float32),
        ),
        in_specs=[pl.BlockSpec(memory_space=pltpu.SMEM), whole, whole],
        out_specs=(whole, whole, whole),
        compiler_params=pltpu.CompilerParams(vmem_limit_bytes=40 * MEBI),
        cost_estimate=pl.CostEstimate(
            flops=9 * 2 * width**3, bytes_accessed=6 * PACKED * SIDE, transcendentals=0
        ),
    )(place, mine, theirs)


def finish(place, ratios, advance, weights, parts, results):
    matrices, rows, width = advance.shape
    pieces = [half for halves, _, _ in parts for half in halves]
    where = [sum(len(halves) for halves, _, _ in parts[:k]) for k in range(len(parts) + 1)]
    count = len(parts)
    middle = width // 2
    scaling = 0.2 * math.sqrt(max(rows * matrices * 2, width))

    def index(step, place):
        chosen = 0
        for k, (_, distance, along) in enumerate(parts):
            below = place[1] == (0 if along else 1)
            signed = jnp.where(below, matrices - distance, distance)
            chosen = jnp.where(step == k, signed, chosen)
        return lax.rem(place[0] + chosen, matrices)

    def kernel(place_ref, ratio_ref, advance_ref, weight_ref, *refs):
        new_weight_ref, update_ref, after_ref = refs[-4:-1]
        after_ref[...] = jnp.zeros_like(after_ref)
        matrix_ref = refs[-1]
        step = pl.program_id(0)
        for k in range(count):

            @pl.when(step == k)
            def _():
                halves = jnp.concatenate([ref[...] for ref in refs[where[k] : where[k + 1]]], axis=0)
                first, second = halves[:HALF], halves[HALF:]
                natural = place_ref[1] == (0 if parts[k][2] else 1)
                packed = jnp.concatenate(
                    [jnp.where(natural, first, second), jnp.where(natural, second, first)], axis=0
                )
                blocks, extra = unpack_blocks(packed, jnp.bfloat16)
                matrix_ref[:middle, :middle] = corner(blocks, 0)
                matrix_ref[:middle, middle:] = off_corner(blocks)
                matrix_ref[middle:width, middle:] = corner(blocks, 2)
                for i in range(4):
                    matrix_ref[width:, i * SIDE : (i + 1) * SIDE] = low(
                        jnp.broadcast_to(extra[4 + i : 5 + i], (16, SIDE))
                    )

        which = index(step, place_ref)
        lane = lax.broadcasted_iota(jnp.int32, (1, SIDE), 1)
        head = (which // 2) * (SIDE * 2 // matrices) + (place_ref[0] * 2 + place_ref[1]) * 2
        row = lax.broadcasted_iota(jnp.int32, (rows, 1), 0)
        factor = jnp.zeros((rows, 1), jnp.float32)
        for k in range(rows // DK):
            ratio = jnp.sum(
                jnp.where(lane == head + k, ratio_ref[...], 0.0), axis=1, keepdims=True
            )
            factor = jnp.where(row // DK == k, ratio, factor)
        factor = jnp.where(which % 2 == 0, factor, 1.0)
        off = matrix_ref[:middle, middle:]
        left, right = advance_ref[0, :, :middle], advance_ref[0, :, middle:]
        halves = (
            jnp.dot(left, matrix_ref[:middle, :middle], preferred_element_type=jnp.float32)
            + lax.dot_general(
                right, off, (((1,), (1,)), ((), ())), preferred_element_type=jnp.float32
            ),
            jnp.dot(left, off, preferred_element_type=jnp.float32)
            + jnp.dot(right, matrix_ref[middle:width, middle:], preferred_element_type=jnp.float32),
        )
        for k, values in enumerate((left, right)):
            columns = slice(k * middle, (k + 1) * middle)
            rest = wide(matrix_ref[width : width + 1, columns])
            scaled = scaling * (halves[k] + wide(values) * rest)
            update_ref[0, :, columns] = low(scaled)
            new_weight = (wide(weight_ref[0, :, columns]) * SHRINK - LEARN_RATE * scaled) * factor
            new_weight_ref[0, :, columns] = low(new_weight)

    full = pl.BlockSpec((1, rows, width), lambda step, place: (index(step, place), 0, 0))
    one_row = pl.BlockSpec((1, SIDE), lambda step, place: (0, 0))
    anywhere = pl.BlockSpec(memory_space=pl.ANY)
    shape = jax.ShapeDtypeStruct(advance.shape, jnp.bfloat16)
    carry = [] if results is None else list(results)
    first_carried = 4 + len(pieces)
    return pl.pallas_call(
        kernel,
        out_shape=(shape, shape, jax.ShapeDtypeStruct((1, SIDE), jnp.bfloat16)),
        grid_spec=pltpu.PrefetchScalarGridSpec(
            num_scalar_prefetch=1,
            grid=(count,),
            in_specs=[one_row, full, full]
            + [pl.BlockSpec(half.shape, lambda step, place: (0, 0)) for half in pieces]
             + [anywhere] * len(carry),
            out_specs=(full, full, one_row),
            scratch_shapes=[pltpu.VMEM((width + 16, width), jnp.bfloat16)],
        ),
        input_output_aliases={first_carried + k: k for k in range(len(carry))},
        compiler_params=pltpu.CompilerParams(vmem_limit_bytes=48 * MEBI),
        cost_estimate=pl.CostEstimate(
            flops=2 * count * rows * width * width,
            bytes_accessed=count * (8 * rows * width + 2 * PACKED * SIDE),
            transcendentals=0,
        ),
    )(place, ratios, advance, weights, *pieces, *carry)


def observed_rows(head_logits, layers):
    parties, observers = lax.axis_size("dp"), lax.axis_size("mp")
    dp = lax.axis_index("dp")
    start = jnp.bitwise_xor(lax.axis_index("mp"), dp) * layers
    pairs = [
        (k * observers + i, k * observers + (i ^ k)) for k in range(parties) for i in range(observers)
    ]
    sent = lax.dynamic_slice_in_dim(head_logits[0], start, layers, 0)
    values = lax.ppermute(sent, ("dp", "mp"), pairs).reshape(1, -1)
    high = lax.reduce_precision(values, 8, 7)
    middle = lax.reduce_precision(values - high, 8, 7)
    rest = values - high - middle
    row = lax.broadcasted_iota(jnp.int32, (GRAM_ROWS - SQUARES, 1), 0)
    kind, slot = row // parties, row % parties
    chosen = jnp.where(kind == 1, high, jnp.where(kind == 2, middle, rest))
    return low(jnp.where(jnp.logical_and(kind > 0, slot == dp), chosen, 0.0))


def shards(gradients, moments, weights, head_logits):
    layers, kind_count, row_count, latent_width = gradients.shape
    matrices = layers * kind_count
    parties = lax.axis_size("dp")
    dp = lax.axis_index("dp")
    core = dp % 2
    place = jnp.stack([dp // 2, core]).astype(jnp.int32)
    stacked = (matrices, row_count, latent_width)

    swap_pairs = [(i, i ^ 1) for i in range(parties)]

    def swap(value):
        return lax.ppermute(value, "dp", swap_pairs)

    def onward(value, distance):
        pairs = [(i, (i + 2 * distance * (1 - 2 * (i % 2))) % parties) for i in range(parties)]
        return lax.ppermute(value, "dp", pairs)

    new_moments, advance, mine, theirs, far_mine, far_theirs, own = grams(
        gradients.reshape(stacked), moments.reshape(stacked)
    )
    rows = observed_rows(head_logits, layers)
    both_rows = wide(rows) + wide(swap(rows))
    far_arrived, arrived = swap(far_theirs), swap(theirs)

    def behind(value, start):
        return jnp.pad(value, ((start, 0), (0, 0)))

    rows_first = behind(jnp.where(core == 0, 0.0, both_rows), SQUARES - GRAM_HALF)
    rows_second = behind(jnp.where(core == 0, both_rows, 0.0), SQUARES - GRAM_HALF)

    def first_half(distance):
        slot = 3 - distance
        return wide(mine[slot, :GRAM_HALF]) + wide(arrived[slot, :GRAM_HALF]) + rows_first

    def second_half(distance):
        slot = 3 - distance
        return wide(mine[slot, GRAM_HALF:]) + wide(arrived[slot, GRAM_HALF:]) + rows_second

    def hop(value):
        return wide(onward(low(value), 1))

    far = low(wide(far_mine) + wide(far_arrived) + rows_first)
    firsts = [first_half(distance) for distance in (3, 2, 1)]
    seconds = [second_half(distance) for distance in (3, 2, 1)]
    firsts[0], seconds[0] = low(firsts[0]), low(seconds[0])
    far, firsts, seconds = lax.optimization_barrier((far, firsts, seconds))
    far = wide(onward(far, 2))
    first, second = wide(onward(firsts[0], 1)), wide(onward(seconds[0], 1))
    first, second = hop(firsts[1] + first + far), hop(seconds[1] + second)
    first, second = hop(firsts[2] + first), hop(seconds[2] + second)
    own_rows = behind(wide(rows), SQUARES - GRAM_HALF)
    first = first + wide(own[:GRAM_HALF]) + jnp.where(core == 0, 0.0, own_rows)
    second = second + wide(own[GRAM_HALF:]) + jnp.where(core == 0, own_rows, 0.0)
    partial = low(jnp.concatenate([first, second], axis=0))

    first, second, ratios = polynomial(place, partial, swap(partial))

    def final(parts, results):
        *results, after = finish(
            place, ratios, advance, weights.reshape(stacked), parts, results
        )
        return results, after

    results, begun = final([((first, second), 0, True)], None)
    parts = []
    for distance in (1, 2, 3):
        first, second = onward(first, 1), onward(second, 1)
        if distance == 2:
            far = onward(first, 2)
        parts.append((first, second))

    def both_ways(halves, distance, before):
        other = swap(jnp.concatenate(halves, axis=0) + before)
        return [(halves, distance, True), ((other,), distance, False)]

    results, after = final(
        both_ways(parts[0], 1, begun) + both_ways(parts[1], 2, begun), results
    )
    far = far + after
    (new_weights, updates), _ = final(
        both_ways(parts[2], 3, after) + [((far, swap(far)), 4, True)], results
    )
    whole = gradients.shape
    return (new_weights.reshape(whole), new_moments.reshape(whole), updates.reshape(whole))


def solution(mesh):
    return jax.shard_map(
        shards,
        mesh=mesh,
        in_specs=(
            P("mp", None, "dp", None),
            P("mp", None, "dp", None),
            P("mp", None, "dp", None),
            P("mp", None, None),
        ),
        out_specs=(P("mp", None, "dp", None), P("mp", None, "dp", None), P("mp", None, "dp", None)),
        check_vma=False,
    )
```

```python
import math

import jax
import jax.numpy as jnp
from jax import lax
from jax.experimental import pallas as pl
from jax.experimental.pallas import tpu as pltpu
from jax.sharding import PartitionSpec as P

DK = 128
SIDE = 128
SQUARES = 8 * SIDE
GRAM_ROWS = SQUARES + 64
GRAM_HALF = GRAM_ROWS // 2
PACKED = SQUARES + 32
HALF = PACKED // 2
MEBI = 1024 * 1024

FIRST_COEFF = 3.4445
SECOND_COEFF = -4.775
THIRD_COEFF = 2.0315
MOMENTUM = 0.95
LEARN_RATE = 0.1
SHRINK = 0.99
CLIP_LIMIT = 100.0
EPSILON = 1e-07


def low(value):
    return value.astype(jnp.bfloat16)


def wide(value):
    return value.astype(jnp.float32)


def product(left, right):
    return jnp.dot(low(left), low(right), preferred_element_type=jnp.float32)


def square_iota(dimension):
    return lax.broadcasted_iota(jnp.int32, (SIDE, SIDE), dimension)


def diagonal_row(block):
    return jnp.sum(jnp.where(square_iota(0) == square_iota(1), block, 0.0), axis=0, keepdims=True)


ORDER = ((0, 1), (0, 2), (0, 3)), ((1, 2), (1, 3), (2, 3))


def pack(blocks, rows, residuals=False, peaks=None):
    upper = square_iota(0) <= square_iota(1)
    pieces = []
    for which in range(2):
        even, odd = blocks[2 * which, 2 * which], blocks[2 * which + 1, 2 * which + 1]
        pieces.append(jnp.where(upper, even, odd))
        pieces += [blocks[name] for name in ORDER[which]]
    row = lax.broadcasted_iota(jnp.int32, (rows - SQUARES, SIDE), 0)
    extra = jnp.zeros(row.shape, jnp.float32)
    for i in range(4):
        values = diagonal_row(blocks[i, i])
        extra = jnp.where(row == i, values, extra)
        if residuals:
            extra = jnp.where(row == 4 + i, values - wide(low(values)), extra)
    if peaks is not None:
        for i in range(3):
            extra = jnp.where(row == 8 + i, peaks, extra)
            peaks = peaks - wide(low(peaks))
    return jnp.concatenate([low(piece) for piece in pieces + [extra]], axis=0)


def unpack_blocks(packed, dtype):
    rows, columns = square_iota(0), square_iota(1)
    extra = wide(packed[SQUARES:])
    blocks = {}
    for which in range(2):
        pieces = [packed[(4 * which + k) * SIDE : (4 * which + k + 1) * SIDE] for k in range(4)]
        both = wide(pieces[0])
        turned = both.T
        first, second = extra[2 * which : 2 * which + 1], extra[2 * which + 1 : 2 * which + 2]
        even = jnp.where(rows < columns, both, jnp.where(rows > columns, turned, first))
        odd = jnp.where(rows > columns, both, jnp.where(rows < columns, turned, second))
        blocks[2 * which, 2 * which] = even.astype(dtype)
        blocks[2 * which + 1, 2 * which + 1] = odd.astype(dtype)
        for name, piece in zip(ORDER[which], pieces[1:]):
            blocks[name] = piece.astype(dtype)
    return blocks, extra


def corner(blocks, i):
    right = blocks[i, i + 1]
    return jnp.concatenate(
        [
            jnp.concatenate([blocks[i, i], right], axis=1),
            jnp.concatenate([wide(right).T.astype(right.dtype), blocks[i + 1, i + 1]], axis=1),
        ],
        axis=0,
    )


def off_corner(blocks):
    return jnp.concatenate(
        [jnp.concatenate([blocks[i, 2], blocks[i, 3]], axis=1) for i in (0, 1)], axis=0
    )


def cut_blocks(matrix):
    return {
        (i, j): matrix[i * SIDE : (i + 1) * SIDE, j * SIDE : (j + 1) * SIDE]
        for i in range(4)
        for j in range(i, 4)
    }


def carried(step):
    return 4 - (step + 1) // 2, (step % 2) == 1


def gram_kernel(
    grad_hbm, moment_hbm,
    new_moment_hbm, advance_hbm, mine_hbm, theirs_hbm, far_mine_hbm, far_theirs_hbm, own_hbm,
    grad_ref, moment_ref, new_moment_ref, advance_ref, packed_ref, in_sems, out_sems,
):
    matrices, rows, width = grad_ref.shape
    dp = lax.axis_index("dp")
    chip, core = dp // 2, dp % 2
    middle = width // 2
    contract = (((0,), (0,)), ((), ()))

    def place_of(step):
        distance, mine = carried(step)
        up = core == (0 if mine else 1)
        return lax.rem(chip + jnp.where(up, distance, matrices - distance), matrices)

    def incoming(step, which):
        source, target = ((grad_hbm, grad_ref), (moment_hbm, moment_ref))[which]
        return pltpu.make_async_copy(
            source.at[place_of(step)], target.at[step], in_sems.at[which, step]
        )

    def outgoing(step, which):
        source, target = ((new_moment_ref, new_moment_hbm), (advance_ref, advance_hbm))[which]
        return pltpu.make_async_copy(
            source.at[step], target.at[place_of(step)], out_sems.at[which, step]
        )

    def packed_copy(source, target, sem):
        return pltpu.make_async_copy(source, target, sem)

    for step in range(matrices):
        incoming(step, 0).start()
        incoming(step, 1).start()
    copies = []
    for step in range(matrices):
        incoming(step, 0).wait()
        incoming(step, 1).wait()
        widened = wide(grad_ref[step])
        moment_sum = MOMENTUM * wide(moment_ref[step]) + widened
        new_moment_ref[step] = low(moment_sum)
        advance = low(widened + MOMENTUM * moment_sum)
        advance_ref[step] = advance
        for which in range(2):
            copies.append(outgoing(step, which))
            copies[-1].start()
        upper = lax.dot_general(
            advance[:, :middle], advance, contract, preferred_element_type=jnp.float32
        )
        lower = lax.dot_general(
            advance[:, middle:], advance[:, middle:], contract, preferred_element_type=jnp.float32
        )
        blocks = {}
        for i in range(2):
            for j in range(i, 4):
                blocks[i, j] = upper[i * SIDE : (i + 1) * SIDE, j * SIDE : (j + 1) * SIDE]
            for j in range(i, 2):
                blocks[i + 2, j + 2] = lower[i * SIDE : (i + 1) * SIDE, j * SIDE : (j + 1) * SIDE]
        packed = pack(blocks, GRAM_ROWS)
        mine = step in (0, matrices - 1) or carried(step)[1]
        natural = core == (0 if mine else 1)
        packed_ref[step, :GRAM_HALF] = jnp.where(natural, packed[:GRAM_HALF], packed[GRAM_HALF:])
        packed_ref[step, GRAM_HALF:] = jnp.where(natural, packed[GRAM_HALF:], packed[:GRAM_HALF])
        if step == 0:
            first, second = packed_ref.at[0, :GRAM_HALF], packed_ref.at[0, GRAM_HALF:]
            copies.append(packed_copy(first, far_mine_hbm, out_sems.at[2, 0]))
            copies[-1].start()
            copies.append(packed_copy(second, far_theirs_hbm, out_sems.at[3, 0]))
            copies[-1].start()
            continue
        if step == matrices - 1:
            target = own_hbm
        elif mine:
            target = mine_hbm.at[(step - 1) // 2]
        else:
            target = theirs_hbm.at[(step - 1) // 2]
        copies.append(packed_copy(packed_ref.at[step], target, out_sems.at[2, step]))
        copies[-1].start()
    for copy in copies:
        copy.wait()


def grams(gradients, moments):
    matrices, rows, width = gradients.shape
    there = pl.BlockSpec(memory_space=pltpu.HBM)
    anywhere = pl.BlockSpec(memory_space=pl.ANY)

    def shape(*sizes):
        return jax.ShapeDtypeStruct(sizes, jnp.bfloat16)

    full = shape(*gradients.shape)
    return pl.pallas_call(
        gram_kernel,
        out_shape=(
            full, full, shape(3, GRAM_ROWS, SIDE), shape(3, GRAM_ROWS, SIDE),
            shape(GRAM_HALF, SIDE), shape(GRAM_HALF, SIDE), shape(GRAM_ROWS, SIDE),
        ),
        in_specs=[there, there],
        out_specs=(there, there) + (anywhere,) * 5,
        scratch_shapes=[pltpu.VMEM(gradients.shape, jnp.bfloat16)] * 4
        + [
            pltpu.VMEM((matrices, GRAM_ROWS, SIDE), jnp.bfloat16),
            pltpu.SemaphoreType.DMA((2, matrices)),
            pltpu.SemaphoreType.DMA((4, matrices)),
        ],
        compiler_params=pltpu.CompilerParams(vmem_limit_bytes=50 * MEBI),
        cost_estimate=pl.CostEstimate(
            flops=2 * gradients.size * width, bytes_accessed=10 * gradients.size, transcendentals=0
        ),
    )(gradients, moments)


def polynomial_kernel(
    place_ref, mine_first, mine_second, theirs_first, theirs_second, first_ref, second_ref
):
    natural = place_ref[1] == 0
    first = wide(mine_first[...]) + wide(theirs_second[...])
    second = wide(mine_second[...]) + wide(theirs_first[...])
    packed = jnp.concatenate(
        [jnp.where(natural, first, second), jnp.where(natural, second, first)], axis=0
    )
    blocks, extra = unpack_blocks(packed, jnp.float32)
    logits = extra[16:32] + extra[32:48] + extra[48:64]
    peaks = jnp.max(logits, axis=0, keepdims=True)
    corners = off_corner(blocks)
    gram = jnp.concatenate(
        [
            jnp.concatenate([corner(blocks, 0), corners], axis=1),
            jnp.concatenate([corners.T, corner(blocks, 2)], axis=1),
        ],
        axis=0,
    )
    width = gram.shape[0]
    rows = lax.broadcasted_iota(jnp.int32, (width, width), 0)
    columns = lax.broadcasted_iota(jnp.int32, (width, width), 1)
    diagonal = rows == columns
    norm = jnp.sqrt(jnp.sum(jnp.where(diagonal, gram, 0.0)))
    scale = 1.0 / (norm + EPSILON)
    gram = gram * scale * scale

    def poly(gram):
        return SECOND_COEFF * gram + THIRD_COEFF * product(gram, gram)

    def following(gram, step):
        inner = FIRST_COEFF * gram + product(gram, step)
        return FIRST_COEFF * inner + product(inner, step)

    rest = poly(gram)
    factor = FIRST_COEFF
    gram = following(gram, rest)
    for last in (False, True):
        step = poly(gram)
        if not last:
            gram = following(gram, step)
        rest = FIRST_COEFF * rest + factor * step + product(rest, step)
        factor = factor * FIRST_COEFF
    total = jnp.where(diagonal, rest + factor, rest) * scale
    packed = pack(cut_blocks(total), PACKED, residuals=True, peaks=peaks)
    first_ref[...] = jnp.where(natural, packed[:HALF], packed[HALF:])
    second_ref[...] = jnp.where(natural, packed[HALF:], packed[:HALF])


def polynomial(place, mine, theirs):
    width = 4 * SIDE
    whole = pl.BlockSpec(memory_space=pltpu.VMEM)
    half = jax.ShapeDtypeStruct((HALF, SIDE), jnp.bfloat16)
    return pl.pallas_call(
        polynomial_kernel,
        out_shape=(half, half),
        in_specs=[pl.BlockSpec(memory_space=pltpu.SMEM)] + [whole] * 4,
        out_specs=(whole, whole),
        compiler_params=pltpu.CompilerParams(vmem_limit_bytes=40 * MEBI),
        cost_estimate=pl.CostEstimate(
            flops=9 * 2 * width**3, bytes_accessed=6 * PACKED * SIDE, transcendentals=0
        ),
    )(place, *mine, *theirs)


def finish(place, peaks, advance, weights, parts, results):
    matrices, rows, width = advance.shape
    pieces = []
    for halves, _, _ in parts:
        for array, _ in halves:
            if not any(array is piece for piece in pieces):
                pieces.append(array)
    places = [
        [([array is piece for piece in pieces].index(True), row) for array, row in halves]
        for halves, _, _ in parts
    ]
    count = len(parts)
    middle = width // 2
    scaling = 0.2 * math.sqrt(max(rows * matrices * 2, width))

    def index(step, place):
        chosen = 0
        for k, (_, distance, along) in enumerate(parts):
            below = place[1] == (0 if along else 1)
            signed = jnp.where(below, matrices - distance, distance)
            chosen = jnp.where(step == k, signed, chosen)
        return lax.rem(place[0] + chosen, matrices)

    def kernel(place_ref, peaks_ref, advance_ref, weight_ref, *refs):
        new_weight_ref, update_ref, peaks_out_ref, after_ref = refs[-5:-1]
        matrix_ref = refs[-1]
        step = pl.program_id(0)

        @pl.when(step == 0)
        def _():
            after_ref[...] = jnp.zeros_like(after_ref)
            known = peaks_ref[...]
            if peaks is None:
                for k in range(count):
                    ends = [wide(refs[i][row + HALF - 32 : row + HALF]) for i, row in places[k]]
                    natural = place_ref[1] == (0 if parts[k][2] else 1)
                    end = jnp.where(natural, ends[1], ends[0])
                    known = jnp.maximum(known, end[8:9] + end[9:10] + end[10:11])
            peaks_out_ref[...] = known

        for k in range(count):

            @pl.when(step == k)
            def _():
                first, second = [refs[i][row : row + HALF] for i, row in places[k]]
                natural = place_ref[1] == (0 if parts[k][2] else 1)
                packed = jnp.concatenate(
                    [jnp.where(natural, first, second), jnp.where(natural, second, first)], axis=0
                )
                blocks, extra = unpack_blocks(packed, jnp.bfloat16)
                matrix_ref[:middle, :middle] = corner(blocks, 0)
                matrix_ref[:middle, middle:] = off_corner(blocks)
                matrix_ref[middle:width, middle:] = corner(blocks, 2)
                for i in range(4):
                    matrix_ref[width:, i * SIDE : (i + 1) * SIDE] = low(
                        jnp.broadcast_to(extra[4 + i : 5 + i], (16, SIDE))
                    )

        which = index(step, place_ref)
        ratios = jnp.sqrt(jnp.minimum(1.0, CLIP_LIMIT / peaks_out_ref[...]))
        lane = lax.broadcasted_iota(jnp.int32, (1, SIDE), 1)
        head = (which // 2) * (SIDE * 2 // matrices) + (place_ref[0] * 2 + place_ref[1]) * 2
        row = lax.broadcasted_iota(jnp.int32, (rows, 1), 0)
        factor = jnp.zeros((rows, 1), jnp.float32)
        for k in range(rows // DK):
            ratio = jnp.sum(
                jnp.where(lane == head + k, ratios, 0.0), axis=1, keepdims=True
            )
            factor = jnp.where(row // DK == k, ratio, factor)
        factor = jnp.where(which % 2 == 0, factor, 1.0)
        off = matrix_ref[:middle, middle:]
        left, right = advance_ref[0, :, :middle], advance_ref[0, :, middle:]
        halves = (
            jnp.dot(left, matrix_ref[:middle, :middle], preferred_element_type=jnp.float32)
            + lax.dot_general(
                right, off, (((1,), (1,)), ((), ())), preferred_element_type=jnp.float32
            ),
            jnp.dot(left, off, preferred_element_type=jnp.float32)
            + jnp.dot(right, matrix_ref[middle:width, middle:], preferred_element_type=jnp.float32),
        )
        for k, values in enumerate((left, right)):
            columns = slice(k * middle, (k + 1) * middle)
            rest = wide(matrix_ref[width : width + 1, columns])
            scaled = scaling * (halves[k] + wide(values) * rest)
            update_ref[0, :, columns] = low(scaled)
            new_weight = (wide(weight_ref[0, :, columns]) * SHRINK - LEARN_RATE * scaled) * factor
            new_weight_ref[0, :, columns] = low(new_weight)

    full = pl.BlockSpec((1, rows, width), lambda step, place: (index(step, place), 0, 0))
    one_row = pl.BlockSpec((1, SIDE), lambda step, place: (0, 0))
    anywhere = pl.BlockSpec(memory_space=pl.ANY)
    shape = jax.ShapeDtypeStruct(advance.shape, jnp.bfloat16)
    carry = [] if results is None else list(results)
    first_carried = 4 + len(pieces)
    return pl.pallas_call(
        kernel,
        out_shape=(
            shape,
            shape,
            jax.ShapeDtypeStruct((1, SIDE), jnp.float32),
            jax.ShapeDtypeStruct((1, SIDE), jnp.bfloat16),
        ),
        grid_spec=pltpu.PrefetchScalarGridSpec(
            num_scalar_prefetch=1,
            grid=(count,),
            in_specs=[one_row, full, full]
            + [pl.BlockSpec(half.shape, lambda step, place: (0, 0)) for half in pieces]
             + [anywhere] * len(carry),
            out_specs=(full, full, one_row, one_row),
            scratch_shapes=[pltpu.VMEM((width + 16, width), jnp.bfloat16)],
        ),
        input_output_aliases={first_carried + k: k for k in range(len(carry))},
        compiler_params=pltpu.CompilerParams(vmem_limit_bytes=48 * MEBI),
        cost_estimate=pl.CostEstimate(
            flops=2 * count * rows * width * width,
            bytes_accessed=count * (8 * rows * width + 2 * PACKED * SIDE),
            transcendentals=0,
        ),
    )(
        place,
        jnp.zeros((1, SIDE), jnp.float32) if peaks is None else peaks,
        advance,
        weights,
        *pieces,
        *carry,
    )


def observed(head_logits, layers):
    parties, observers = lax.axis_size("dp"), lax.axis_size("mp")
    dp = lax.axis_index("dp")
    start = jnp.bitwise_xor(lax.axis_index("mp"), dp) * layers
    pairs = [
        (k * observers + i, k * observers + (i ^ k)) for k in range(parties) for i in range(observers)
    ]
    sent = lax.dynamic_slice_in_dim(head_logits[0], start, layers, 0)
    return lax.ppermute(sent, ("dp", "mp"), pairs).reshape(1, -1)


def gram_rows(values):
    parties = lax.axis_size("dp")
    dp = lax.axis_index("dp")
    high = lax.reduce_precision(values, 8, 7)
    middle = lax.reduce_precision(values - high, 8, 7)
    rest = values - high - middle
    row = lax.broadcasted_iota(jnp.int32, (GRAM_ROWS - SQUARES, 1), 0)
    kind, slot = row // parties, row % parties
    chosen = jnp.where(kind == 1, high, jnp.where(kind == 2, middle, rest))
    return low(jnp.where(jnp.logical_and(kind > 0, slot == dp), chosen, 0.0))


def shards(gradients, moments, weights, head_logits):
    layers, kind_count, row_count, latent_width = gradients.shape
    matrices = layers * kind_count
    parties = lax.axis_size("dp")
    dp = lax.axis_index("dp")
    core = dp % 2
    place = jnp.stack([dp // 2, core]).astype(jnp.int32)
    stacked = (matrices, row_count, latent_width)

    swap_pairs = [(i, i ^ 1) for i in range(parties)]

    def swap(value):
        return lax.ppermute(value, "dp", swap_pairs)

    def onward(value, distance):
        pairs = [(i, (i + 2 * distance * (1 - 2 * (i % 2))) % parties) for i in range(parties)]
        return lax.ppermute(value, "dp", pairs)

    new_moments, advance, mine, theirs, far_mine, far_theirs, own = grams(
        gradients.reshape(stacked), moments.reshape(stacked)
    )
    far_arrived, arrived = swap(far_theirs), swap(theirs)

    def first_half(distance):
        slot = 3 - distance
        return wide(mine[slot, :GRAM_HALF]) + wide(arrived[slot, :GRAM_HALF])

    def second_half(distance):
        slot = 3 - distance
        return wide(mine[slot, GRAM_HALF:]) + wide(arrived[slot, GRAM_HALF:])

    def in_first(rows):
        rows = jnp.where(core == 0, 0.0, wide(rows))
        return jnp.pad(rows, ((SQUARES - GRAM_HALF, 0), (0, 0)))

    def in_second(rows):
        rows = jnp.where(core == 0, wide(rows), 0.0)
        return jnp.pad(rows, ((SQUARES - GRAM_HALF, 0), (0, 0)))

    def hop(value):
        return wide(onward(low(value), 1))

    far = low(wide(far_mine) + wide(far_arrived))
    firsts = [first_half(distance) for distance in (3, 2, 1)]
    seconds = [second_half(distance) for distance in (3, 2, 1)]
    firsts[0], seconds[0] = low(firsts[0]), low(seconds[0])
    far, firsts, seconds, head_logits = lax.optimization_barrier(
        (far, firsts, seconds, head_logits)
    )
    values = observed(head_logits, layers)
    far = wide(onward(far, 2))
    first, second = wide(onward(firsts[0], 1)), wide(onward(seconds[0], 1))
    values, far, first, second = lax.optimization_barrier((values, far, first, second))
    rows = gram_rows(values)
    first, second = (
        hop(firsts[1] + first + far + in_first(rows)),
        hop(seconds[1] + second + in_second(rows)),
    )
    both_rows = lax.optimization_barrier(rows) + lax.optimization_barrier(swap(rows))
    first, second = (
        hop(firsts[2] + first + in_first(both_rows)),
        hop(seconds[2] + second + in_second(both_rows)),
    )
    second = low(second + wide(own[GRAM_HALF:]) + in_second(rows))
    first = low(first + wide(own[:GRAM_HALF]) + in_first(rows))
    first, second = polynomial(place, (first, second), (swap(first), swap(second)))

    def final(peaks, parts, results):
        *results, peaks, after = finish(
            place, peaks, advance, weights.reshape(stacked), parts, results
        )
        return results, peaks, after

    pieces = [(first, second)]
    for distance in (1, 2, 3):
        first, second = onward(first, 1), onward(second, 1)
        if distance == 2:
            far = onward(first, 2)
        pieces.append((first, second))
    near = [half for halves in pieces[1:3] for half in halves]
    other_near = swap(jnp.concatenate(near, axis=0))
    results, peaks, after = final(
        None,
        [
            ([(half, 0) for half in pieces[0]], 0, True),
            ([(half, 0) for half in pieces[1]], 1, True),
            ([(other_near, 0), (other_near, HALF)], 1, False),
            ([(half, 0) for half in pieces[2]], 2, True),
            ([(other_near, 2 * HALF), (other_near, 3 * HALF)], 2, False),
        ],
        None,
    )
    other_remote = swap(jnp.concatenate([*pieces[3], far], axis=0) + after)
    (new_weights, updates), _, _ = final(
        peaks,
        [
            ([(half, 0) for half in pieces[3]], 3, True),
            ([(other_remote, 0), (other_remote, HALF)], 3, False),
            ([(far, 0), (other_remote, 2 * HALF)], 4, True),
        ],
        results,
    )
    whole = gradients.shape
    return (new_weights.reshape(whole), new_moments.reshape(whole), updates.reshape(whole))


def solution(mesh):
    return jax.shard_map(
        shards,
        mesh=mesh,
        in_specs=(
            P("mp", None, "dp", None),
            P("mp", None, "dp", None),
            P("mp", None, "dp", None),
            P("mp", None, None),
        ),
        out_specs=(P("mp", None, "dp", None), P("mp", None, "dp", None), P("mp", None, "dp", None)),
        check_vma=False,
    )
```

```python
import functools
import math

import jax
import jax.numpy as jnp
from jax import lax
from jax.experimental import pallas as pl
from jax.experimental.pallas import tpu as pltpu
from jax.sharding import PartitionSpec as P

DK = 128
SIDE = 128
SQUARES = 8 * SIDE
GRAM_ROWS = SQUARES + 64
GRAM_HALF = GRAM_ROWS // 2
PACKED = SQUARES + 32
HALF = PACKED // 2
MEBI = 1024 * 1024

FIRST_COEFF = 3.4445
SECOND_COEFF = -4.775
THIRD_COEFF = 2.0315
MOMENTUM = 0.95
LEARN_RATE = 0.1
SHRINK = 0.99
CLIP_LIMIT = 100.0
EPSILON = 1e-07


def low(value):
    return value.astype(jnp.bfloat16)


def wide(value):
    return value.astype(jnp.float32)


def product(left, right):
    return jnp.dot(low(left), low(right), preferred_element_type=jnp.float32)


def square_iota(dimension):
    return lax.broadcasted_iota(jnp.int32, (SIDE, SIDE), dimension)


def diagonal_row(block):
    return jnp.sum(jnp.where(square_iota(0) == square_iota(1), block, 0.0), axis=0, keepdims=True)


ORDER = ((0, 1), (0, 2), (0, 3)), ((1, 2), (1, 3), (2, 3))


def pack(blocks, rows, residuals=False, peaks=None):
    upper = square_iota(0) <= square_iota(1)
    pieces = []
    for which in range(2):
        even, odd = blocks[2 * which, 2 * which], blocks[2 * which + 1, 2 * which + 1]
        pieces.append(jnp.where(upper, even, odd))
        pieces += [blocks[name] for name in ORDER[which]]
    row = lax.broadcasted_iota(jnp.int32, (rows - SQUARES, SIDE), 0)
    extra = jnp.zeros(row.shape, jnp.float32)
    for i in range(4):
        values = diagonal_row(blocks[i, i])
        extra = jnp.where(row == i, values, extra)
        if residuals:
            extra = jnp.where(row == 4 + i, values - wide(low(values)), extra)
    if peaks is not None:
        for i in range(3):
            extra = jnp.where(row == 8 + i, peaks, extra)
            peaks = peaks - wide(low(peaks))
    return jnp.concatenate([low(piece) for piece in pieces + [extra]], axis=0)


def unpack_blocks(packed, dtype):
    rows, columns = square_iota(0), square_iota(1)
    extra = wide(packed[SQUARES:])
    blocks = {}
    for which in range(2):
        pieces = [packed[(4 * which + k) * SIDE : (4 * which + k + 1) * SIDE] for k in range(4)]
        both = wide(pieces[0])
        turned = both.T
        first, second = extra[2 * which : 2 * which + 1], extra[2 * which + 1 : 2 * which + 2]
        even = jnp.where(rows < columns, both, jnp.where(rows > columns, turned, first))
        odd = jnp.where(rows > columns, both, jnp.where(rows < columns, turned, second))
        blocks[2 * which, 2 * which] = even.astype(dtype)
        blocks[2 * which + 1, 2 * which + 1] = odd.astype(dtype)
        for name, piece in zip(ORDER[which], pieces[1:]):
            blocks[name] = piece.astype(dtype)
    return blocks, extra


def corner(blocks, i):
    right = blocks[i, i + 1]
    return jnp.concatenate(
        [
            jnp.concatenate([blocks[i, i], right], axis=1),
            jnp.concatenate([wide(right).T.astype(right.dtype), blocks[i + 1, i + 1]], axis=1),
        ],
        axis=0,
    )


def off_corner(blocks):
    return jnp.concatenate(
        [jnp.concatenate([blocks[i, 2], blocks[i, 3]], axis=1) for i in (0, 1)], axis=0
    )


def cut_blocks(matrix):
    return {
        (i, j): matrix[i * SIDE : (i + 1) * SIDE, j * SIDE : (j + 1) * SIDE]
        for i in range(4)
        for j in range(i, 4)
    }


def carried(step):
    return 4 - (step + 1) // 2, (step % 2) == 1


def gram_kernel(steps, matrices, grad_hbm, moment_hbm, *refs):
    new_moment_hbm, advance_hbm, ours_hbm, theirs_hbm = refs[-11:-7]
    grad_ref, moment_ref, new_moment_ref, advance_ref, packed_ref, in_sems, out_sems = refs[-7:]
    own_hbm = ours_hbm.at[pl.ds(2 * GRAM_ROWS, GRAM_ROWS)] if steps[-1] == matrices - 1 else None
    width = grad_ref.shape[2]
    dp = lax.axis_index("dp")
    chip, core = dp // 2, dp % 2
    middle = width // 2
    contract = (((0,), (0,)), ((), ()))

    def place_of(step):
        distance, mine = carried(step)
        up = core == (0 if mine else 1)
        return lax.rem(chip + jnp.where(up, distance, matrices - distance), matrices)

    def incoming(k, which):
        source, target = ((grad_hbm, grad_ref), (moment_hbm, moment_ref))[which]
        return pltpu.make_async_copy(
            source.at[place_of(steps[k])], target.at[k], in_sems.at[which, k]
        )

    def outgoing(k, which):
        source, target = ((new_moment_ref, new_moment_hbm), (advance_ref, advance_hbm))[which]
        return pltpu.make_async_copy(
            source.at[k], target.at[place_of(steps[k])], out_sems.at[which, k]
        )

    for k in range(len(steps)):
        incoming(k, 0).start()
        incoming(k, 1).start()
    copies = []
    for k, step in enumerate(steps):
        incoming(k, 0).wait()
        incoming(k, 1).wait()
        widened = wide(grad_ref[k])
        moment_sum = MOMENTUM * wide(moment_ref[k]) + widened
        new_moment_ref[k] = low(moment_sum)
        advance = low(widened + MOMENTUM * moment_sum)
        advance_ref[k] = advance
        for which in range(2):
            copies.append(outgoing(k, which))
            copies[-1].start()
        upper = lax.dot_general(
            advance[:, :middle], advance, contract, preferred_element_type=jnp.float32
        )
        lower = lax.dot_general(
            advance[:, middle:], advance[:, middle:], contract, preferred_element_type=jnp.float32
        )
        blocks = {}
        for i in range(2):
            for j in range(i, 4):
                blocks[i, j] = upper[i * SIDE : (i + 1) * SIDE, j * SIDE : (j + 1) * SIDE]
            for j in range(i, 2):
                blocks[i + 2, j + 2] = lower[i * SIDE : (i + 1) * SIDE, j * SIDE : (j + 1) * SIDE]
        packed = pack(blocks, GRAM_ROWS)
        distance, mine = carried(step)
        mine = mine or step == 0
        natural = core == (0 if mine else 1)
        packed_ref[k, :GRAM_HALF] = jnp.where(natural, packed[:GRAM_HALF], packed[GRAM_HALF:])
        packed_ref[k, GRAM_HALF:] = jnp.where(natural, packed[GRAM_HALF:], packed[:GRAM_HALF])
        if step == 0:
            moves = [
                (packed_ref.at[k, :GRAM_HALF], ours_hbm.at[pl.ds(0, GRAM_HALF)]),
                (packed_ref.at[k, GRAM_HALF:], theirs_hbm.at[pl.ds(0, GRAM_HALF)]),
            ]
        elif step == matrices - 1:
            moves = [(packed_ref.at[k], own_hbm)]
        else:
            start = {3: GRAM_HALF, 2: 0, 1: GRAM_ROWS}[distance]
            target = ours_hbm if mine else theirs_hbm
            moves = [(packed_ref.at[k], target.at[pl.ds(start, GRAM_ROWS)])]
        for i, (source, target) in enumerate(moves):
            copies.append(pltpu.make_async_copy(source, target, out_sems.at[2 + i, k]))
            copies[-1].start()
    for copy in copies:
        copy.wait()


def grams(gradients, moments, steps, earlier=None, before=None):
    matrices, rows, width = gradients.shape
    anywhere = pl.BlockSpec(memory_space=pl.ANY)
    last = steps[-1] == matrices - 1
    our_rows = 3 * GRAM_ROWS if last else GRAM_HALF + GRAM_ROWS
    their_rows = 2 * GRAM_ROWS if last else GRAM_HALF + GRAM_ROWS
    full = jax.ShapeDtypeStruct(gradients.shape, jnp.bfloat16)
    some = pltpu.VMEM((len(steps), rows, width), jnp.bfloat16)
    given = [] if earlier is None else [before, *earlier]
    return pl.pallas_call(
        functools.partial(gram_kernel, steps, matrices),
        out_shape=(
            full,
            full,
            jax.ShapeDtypeStruct((our_rows, SIDE), jnp.bfloat16),
            jax.ShapeDtypeStruct((their_rows, SIDE), jnp.bfloat16),
        ),
        in_specs=[anywhere] * (2 + len(given)),
        out_specs=(anywhere,) * 4,
        input_output_aliases={3: 0, 4: 1} if given else {},
        scratch_shapes=[some] * 4
        + [
            pltpu.VMEM((len(steps), GRAM_ROWS, SIDE), jnp.bfloat16),
            pltpu.SemaphoreType.DMA((2, len(steps))),
            pltpu.SemaphoreType.DMA((4, len(steps))),
        ],
        compiler_params=pltpu.CompilerParams(vmem_limit_bytes=50 * MEBI),
        cost_estimate=pl.CostEstimate(
            flops=2 * len(steps) * rows * width * width,
            bytes_accessed=10 * len(steps) * rows * width,
            transcendentals=0,
        ),
    )(gradients, moments, *given)


def polynomial_kernel(
    place_ref, mine_first, mine_second, theirs_first, theirs_second, first_ref, second_ref
):
    natural = place_ref[1] == 0
    first = wide(mine_first[...]) + wide(theirs_second[...])
    second = wide(mine_second[...]) + wide(theirs_first[...])
    packed = jnp.concatenate(
        [jnp.where(natural, first, second), jnp.where(natural, second, first)], axis=0
    )
    blocks, extra = unpack_blocks(packed, jnp.float32)
    logits = extra[16:32] + extra[32:48] + extra[48:64]
    peaks = jnp.max(logits, axis=0, keepdims=True)
    corners = off_corner(blocks)
    gram = jnp.concatenate(
        [
            jnp.concatenate([corner(blocks, 0), corners], axis=1),
            jnp.concatenate([corners.T, corner(blocks, 2)], axis=1),
        ],
        axis=0,
    )
    width = gram.shape[0]
    rows = lax.broadcasted_iota(jnp.int32, (width, width), 0)
    columns = lax.broadcasted_iota(jnp.int32, (width, width), 1)
    diagonal = rows == columns
    norm = jnp.sqrt(jnp.sum(jnp.where(diagonal, gram, 0.0)))
    scale = 1.0 / (norm + EPSILON)
    gram = gram * scale * scale

    def poly(gram):
        return SECOND_COEFF * gram + THIRD_COEFF * product(gram, gram)

    def following(gram, step):
        inner = FIRST_COEFF * gram + product(gram, step)
        return FIRST_COEFF * inner + product(inner, step)

    rest = poly(gram)
    factor = FIRST_COEFF
    gram = following(gram, rest)
    for last in (False, True):
        step = poly(gram)
        if not last:
            gram = following(gram, step)
        rest = FIRST_COEFF * rest + factor * step + product(rest, step)
        factor = factor * FIRST_COEFF
    total = jnp.where(diagonal, rest + factor, rest) * scale
    packed = pack(cut_blocks(total), PACKED, residuals=True, peaks=peaks)
    first_ref[...] = jnp.where(natural, packed[:HALF], packed[HALF:])
    second_ref[...] = jnp.where(natural, packed[HALF:], packed[:HALF])


def polynomial(place, mine, theirs):
    width = 4 * SIDE
    whole = pl.BlockSpec(memory_space=pltpu.VMEM)
    half = jax.ShapeDtypeStruct((HALF, SIDE), jnp.bfloat16)
    return pl.pallas_call(
        polynomial_kernel,
        out_shape=(half, half),
        in_specs=[pl.BlockSpec(memory_space=pltpu.SMEM)] + [whole] * 4,
        out_specs=(whole, whole),
        compiler_params=pltpu.CompilerParams(vmem_limit_bytes=40 * MEBI),
        cost_estimate=pl.CostEstimate(
            flops=9 * 2 * width**3, bytes_accessed=6 * PACKED * SIDE, transcendentals=0
        ),
    )(place, *mine, *theirs)


def finish(place, peaks, advance, weights, parts, results):
    matrices, rows, width = advance.shape
    pieces = []
    for halves, _, _ in parts:
        for array, _ in halves:
            if not any(array is piece for piece in pieces):
                pieces.append(array)
    places = [
        [([array is piece for piece in pieces].index(True), row) for array, row in halves]
        for halves, _, _ in parts
    ]
    count = len(parts)
    middle = width // 2
    scaling = 0.2 * math.sqrt(max(rows * matrices * 2, width))

    def index(step, place):
        chosen = 0
        for k, (_, distance, along) in enumerate(parts):
            below = place[1] == (0 if along else 1)
            signed = jnp.where(below, matrices - distance, distance)
            chosen = jnp.where(step == k, signed, chosen)
        return lax.rem(place[0] + chosen, matrices)

    def kernel(place_ref, peaks_ref, advance_ref, weight_ref, *refs):
        new_weight_ref, update_ref, peaks_out_ref, after_ref = refs[-5:-1]
        matrix_ref = refs[-1]
        step = pl.program_id(0)

        @pl.when(step == 0)
        def _():
            after_ref[...] = jnp.zeros_like(after_ref)
            known = peaks_ref[...]
            if peaks is None:
                for k in range(count):
                    ends = [wide(refs[i][row + HALF - 32 : row + HALF]) for i, row in places[k]]
                    natural = place_ref[1] == (0 if parts[k][2] else 1)
                    end = jnp.where(natural, ends[1], ends[0])
                    known = jnp.maximum(known, end[8:9] + end[9:10] + end[10:11])
            peaks_out_ref[...] = known

        for k in range(count):

            @pl.when(step == k)
            def _():
                first, second = [refs[i][row : row + HALF] for i, row in places[k]]
                natural = place_ref[1] == (0 if parts[k][2] else 1)
                packed = jnp.concatenate(
                    [jnp.where(natural, first, second), jnp.where(natural, second, first)], axis=0
                )
                blocks, extra = unpack_blocks(packed, jnp.bfloat16)
                matrix_ref[:middle, :middle] = corner(blocks, 0)
                matrix_ref[:middle, middle:] = off_corner(blocks)
                matrix_ref[middle:width, middle:] = corner(blocks, 2)
                for i in range(4):
                    matrix_ref[width:, i * SIDE : (i + 1) * SIDE] = low(
                        jnp.broadcast_to(extra[4 + i : 5 + i], (16, SIDE))
                    )

        which = index(step, place_ref)
        ratios = jnp.sqrt(jnp.minimum(1.0, CLIP_LIMIT / peaks_out_ref[...]))
        lane = lax.broadcasted_iota(jnp.int32, (1, SIDE), 1)
        head = (which // 2) * (SIDE * 2 // matrices) + (place_ref[0] * 2 + place_ref[1]) * 2
        row = lax.broadcasted_iota(jnp.int32, (rows, 1), 0)
        factor = jnp.zeros((rows, 1), jnp.float32)
        for k in range(rows // DK):
            ratio = jnp.sum(
                jnp.where(lane == head + k, ratios, 0.0), axis=1, keepdims=True
            )
            factor = jnp.where(row // DK == k, ratio, factor)
        factor = jnp.where(which % 2 == 0, factor, 1.0)
        off = matrix_ref[:middle, middle:]
        left, right = advance_ref[which, :, :middle], advance_ref[which, :, middle:]
        halves = (
            jnp.dot(left, matrix_ref[:middle, :middle], preferred_element_type=jnp.float32)
            + lax.dot_general(
                right, off, (((1,), (1,)), ((), ())), preferred_element_type=jnp.float32
            ),
            jnp.dot(left, off, preferred_element_type=jnp.float32)
            + jnp.dot(right, matrix_ref[middle:width, middle:], preferred_element_type=jnp.float32),
        )
        for k, values in enumerate((left, right)):
            columns = slice(k * middle, (k + 1) * middle)
            rest = wide(matrix_ref[width : width + 1, columns])
            scaled = scaling * (halves[k] + wide(values) * rest)
            update_ref[0, :, columns] = low(scaled)
            new_weight = (wide(weight_ref[which, :, columns]) * SHRINK - LEARN_RATE * scaled) * factor
            new_weight_ref[0, :, columns] = low(new_weight)

    full = pl.BlockSpec((1, rows, width), lambda step, place: (index(step, place), 0, 0))
    held = pl.BlockSpec(memory_space=pltpu.VMEM)
    one_row = pl.BlockSpec((1, SIDE), lambda step, place: (0, 0))
    anywhere = pl.BlockSpec(memory_space=pl.ANY)
    shape = jax.ShapeDtypeStruct(advance.shape, jnp.bfloat16)
    carry = [] if results is None else list(results)
    first_carried = 4 + len(pieces)
    return pl.pallas_call(
        kernel,
        out_shape=(
            shape,
            shape,
            jax.ShapeDtypeStruct((1, SIDE), jnp.float32),
            jax.ShapeDtypeStruct((1, SIDE), jnp.bfloat16),
        ),
        grid_spec=pltpu.PrefetchScalarGridSpec(
            num_scalar_prefetch=1,
            grid=(count,),
            in_specs=[one_row, held, held]
            + [pl.BlockSpec(half.shape, lambda step, place: (0, 0)) for half in pieces]
             + [anywhere] * len(carry),
            out_specs=(full, full, one_row, one_row),
            scratch_shapes=[pltpu.VMEM((width + 16, width), jnp.bfloat16)],
        ),
        input_output_aliases={first_carried + k: k for k in range(len(carry))},
        compiler_params=pltpu.CompilerParams(vmem_limit_bytes=48 * MEBI),
        cost_estimate=pl.CostEstimate(
            flops=2 * count * rows * width * width,
            bytes_accessed=count * (8 * rows * width + 2 * PACKED * SIDE),
            transcendentals=0,
        ),
    )(
        place,
        jnp.zeros((1, SIDE), jnp.float32) if peaks is None else peaks,
        advance,
        weights,
        *pieces,
        *carry,
    )


def observed(head_logits, layers):
    parties, observers = lax.axis_size("dp"), lax.axis_size("mp")
    dp = lax.axis_index("dp")
    start = jnp.bitwise_xor(lax.axis_index("mp"), dp) * layers
    pairs = [
        (k * observers + i, k * observers + (i ^ k)) for k in range(parties) for i in range(observers)
    ]
    sent = lax.dynamic_slice_in_dim(head_logits[0], start, layers, 0)
    return lax.ppermute(sent, ("dp", "mp"), pairs).reshape(1, -1)


def gram_rows(values):
    parties = lax.axis_size("dp")
    dp = lax.axis_index("dp")
    high = lax.reduce_precision(values, 8, 7)
    middle = lax.reduce_precision(values - high, 8, 7)
    rest = values - high - middle
    row = lax.broadcasted_iota(jnp.int32, (GRAM_ROWS - SQUARES, 1), 0)
    kind, slot = row // parties, row % parties
    chosen = jnp.where(kind == 1, high, jnp.where(kind == 2, middle, rest))
    return low(jnp.where(jnp.logical_and(kind > 0, slot == dp), chosen, 0.0))


def shards(gradients, moments, weights, head_logits):
    layers, kind_count, row_count, latent_width = gradients.shape
    matrices = layers * kind_count
    parties = lax.axis_size("dp")
    dp = lax.axis_index("dp")
    core = dp % 2
    place = jnp.stack([dp // 2, core]).astype(jnp.int32)
    stacked = (matrices, row_count, latent_width)

    swap_pairs = [(i, i ^ 1) for i in range(parties)]

    def swap(value):
        return lax.ppermute(value, "dp", swap_pairs)

    def onward(value, distance):
        pairs = [(i, (i + 2 * distance * (1 - 2 * (i % 2))) % parties) for i in range(parties)]
        return lax.ppermute(value, "dp", pairs)

    gradients, moments = gradients.reshape(stacked), moments.reshape(stacked)
    *earlier, ours, theirs = grams(gradients, moments, (0, 1, 2))
    summed = wide(ours) + wide(swap(theirs))
    far = low(summed[:GRAM_HALF])
    first = low(summed[GRAM_HALF : 2 * GRAM_HALF])
    second = low(summed[2 * GRAM_HALF :])
    far, first, second, head_logits = lax.optimization_barrier((far, first, second, head_logits))
    new_moments, advance, ours, theirs = grams(
        gradients, moments, (3, 4, 5, 6, 7), earlier, far
    )

    def in_first(rows):
        rows = jnp.where(core == 0, 0.0, wide(rows))
        return jnp.pad(rows, ((SQUARES - GRAM_HALF, 0), (0, 0)))

    def in_second(rows):
        rows = jnp.where(core == 0, wide(rows), 0.0)
        return jnp.pad(rows, ((SQUARES - GRAM_HALF, 0), (0, 0)))

    def hop(value):
        return wide(onward(low(value), 1))

    values = observed(head_logits, layers)
    far = wide(onward(far, 2))
    first, second = wide(onward(first, 1)), wide(onward(second, 1))
    summed = wide(ours[: 2 * GRAM_ROWS]) + wide(swap(theirs))
    own = wide(ours[2 * GRAM_ROWS :])
    halves = [summed[k * GRAM_HALF : (k + 1) * GRAM_HALF] for k in range(4)]
    halves = lax.optimization_barrier(halves)
    values, far, first, second = lax.optimization_barrier((values, far, first, second))
    rows = gram_rows(values)
    first, second = (
        hop(halves[0] + first + far + in_first(rows)),
        hop(halves[1] + second + in_second(rows)),
    )
    both_rows = lax.optimization_barrier(rows) + lax.optimization_barrier(swap(rows))
    first, second = (
        hop(halves[2] + first + in_first(both_rows)),
        hop(halves[3] + second + in_second(both_rows)),
    )
    second = low(second + own[GRAM_HALF:] + in_second(rows))
    first = low(first + own[:GRAM_HALF] + in_first(rows))
    first, second = polynomial(place, (first, second), (swap(first), swap(second)))

    def final(peaks, parts, results):
        *results, peaks, after = finish(
            place, peaks, advance, weights.reshape(stacked), parts, results
        )
        return results, peaks, after

    pieces = [(first, second)]
    for distance in (1, 2, 3):
        first, second = onward(first, 1), onward(second, 1)
        if distance == 2:
            far = onward(first, 2)
        pieces.append((first, second))
    near = [half for halves in pieces[1:3] for half in halves]
    other_near = swap(jnp.concatenate(near, axis=0))
    results, peaks, after = final(
        None,
        [
            ([(half, 0) for half in pieces[0]], 0, True),
            ([(half, 0) for half in pieces[1]], 1, True),
            ([(other_near, 0), (other_near, HALF)], 1, False),
            ([(half, 0) for half in pieces[2]], 2, True),
            ([(other_near, 2 * HALF), (other_near, 3 * HALF)], 2, False),
        ],
        None,
    )
    other_remote = swap(jnp.concatenate([*pieces[3], far], axis=0) + after)
    results, _, _ = final(peaks, [([(half, 0) for half in pieces[3]], 3, True)], results)
    (new_weights, updates), _, _ = final(
        peaks,
        [
            ([(other_remote, 0), (other_remote, HALF)], 3, False),
            ([(far, 0), (other_remote, 2 * HALF)], 4, True),
        ],
        results,
    )
    whole = weights.shape
    return (new_weights.reshape(whole), new_moments.reshape(whole), updates.reshape(whole))


def solution(mesh):
    return jax.shard_map(
        shards,
        mesh=mesh,
        in_specs=(
            P("mp", None, "dp", None),
            P("mp", None, "dp", None),
            P("mp", None, "dp", None),
            P("mp", None, None),
        ),
        out_specs=(P("mp", None, "dp", None), P("mp", None, "dp", None), P("mp", None, "dp", None)),
        check_vma=False,
    )
```

```python
import functools
import math

import jax
import jax.numpy as jnp
from jax import lax
from jax.experimental import pallas as pl
from jax.experimental.pallas import tpu as pltpu
from jax.sharding import PartitionSpec as P

DK = 128
SIDE = 128
SQUARES = 8 * SIDE
GRAM_ROWS = SQUARES + 64
GRAM_HALF = GRAM_ROWS // 2
PACKED = SQUARES + 32
HALF = PACKED // 2
MEBI = 1024 * 1024

FIRST_COEFF = 3.4445
SECOND_COEFF = -4.775
THIRD_COEFF = 2.0315
MOMENTUM = 0.95
LEARN_RATE = 0.1
SHRINK = 0.99
CLIP_LIMIT = 100.0
EPSILON = 1e-07


def low(value):
    return value.astype(jnp.bfloat16)


def wide(value):
    return value.astype(jnp.float32)


def product(left, right):
    return jnp.dot(low(left), low(right), preferred_element_type=jnp.float32)


def square_iota(dimension):
    return lax.broadcasted_iota(jnp.int32, (SIDE, SIDE), dimension)


def diagonal_row(block):
    return jnp.sum(jnp.where(square_iota(0) == square_iota(1), block, 0.0), axis=0, keepdims=True)


ORDER = ((0, 1), (0, 2), (0, 3)), ((1, 2), (1, 3), (2, 3))


def pack(blocks, rows, residuals=False):
    upper = square_iota(0) <= square_iota(1)
    pieces = []
    for which in range(2):
        even, odd = blocks[2 * which, 2 * which], blocks[2 * which + 1, 2 * which + 1]
        pieces.append(jnp.where(upper, even, odd))
        pieces += [blocks[name] for name in ORDER[which]]
    row = lax.broadcasted_iota(jnp.int32, (rows - SQUARES, SIDE), 0)
    extra = jnp.zeros(row.shape, jnp.float32)
    for i in range(4):
        values = diagonal_row(blocks[i, i])
        extra = jnp.where(row == i, values, extra)
        if residuals:
            extra = jnp.where(row == 4 + i, values - wide(low(values)), extra)
    return jnp.concatenate([low(piece) for piece in pieces + [extra]], axis=0)


def unpack_blocks(packed, dtype):
    rows, columns = square_iota(0), square_iota(1)
    extra = wide(packed[SQUARES:])
    blocks = {}
    for which in range(2):
        pieces = [packed[(4 * which + k) * SIDE : (4 * which + k + 1) * SIDE] for k in range(4)]
        both = wide(pieces[0])
        turned = both.T
        first, second = extra[2 * which : 2 * which + 1], extra[2 * which + 1 : 2 * which + 2]
        even = jnp.where(rows < columns, both, jnp.where(rows > columns, turned, first))
        odd = jnp.where(rows > columns, both, jnp.where(rows < columns, turned, second))
        blocks[2 * which, 2 * which] = even.astype(dtype)
        blocks[2 * which + 1, 2 * which + 1] = odd.astype(dtype)
        for name, piece in zip(ORDER[which], pieces[1:]):
            blocks[name] = piece.astype(dtype)
    return blocks, extra


def corner(blocks, i):
    right = blocks[i, i + 1]
    return jnp.concatenate(
        [
            jnp.concatenate([blocks[i, i], right], axis=1),
            jnp.concatenate([wide(right).T.astype(right.dtype), blocks[i + 1, i + 1]], axis=1),
        ],
        axis=0,
    )


def off_corner(blocks):
    return jnp.concatenate(
        [jnp.concatenate([blocks[i, 2], blocks[i, 3]], axis=1) for i in (0, 1)], axis=0
    )


def cut_blocks(matrix):
    return {
        (i, j): matrix[i * SIDE : (i + 1) * SIDE, j * SIDE : (j + 1) * SIDE]
        for i in range(4)
        for j in range(i, 4)
    }


def carried(step):
    return 4 - (step + 1) // 2, (step % 2) == 1


def gram_kernel(matrices, grad_hbm, moment_hbm, *refs):
    new_moment_hbm, advance_hbm, ours_hbm, theirs_hbm = refs[:4]
    grad_ref, moment_ref, new_moment_ref, advance_ref, packed_ref, in_sems, out_sems = refs[4:]
    width = grad_ref.shape[2]
    dp = lax.axis_index("dp")
    chip, core = dp // 2, dp % 2
    middle = width // 2
    contract = (((0,), (0,)), ((), ()))

    def place_of(step):
        distance, mine = carried(step)
        up = core == (0 if mine else 1)
        return lax.rem(chip + jnp.where(up, distance, matrices - distance), matrices)

    def incoming(k, which):
        source, target = ((grad_hbm, grad_ref), (moment_hbm, moment_ref))[which]
        return pltpu.make_async_copy(
            source.at[place_of(k)], target.at[k], in_sems.at[which, k]
        )

    def outgoing(k, which):
        source, target = ((new_moment_ref, new_moment_hbm), (advance_ref, advance_hbm))[which]
        return pltpu.make_async_copy(
            source.at[k], target.at[place_of(k)], out_sems.at[which, k]
        )

    for k in range(matrices):
        incoming(k, 0).start()
        incoming(k, 1).start()
    copies = []
    for k in range(matrices):
        incoming(k, 0).wait()
        incoming(k, 1).wait()
        widened = wide(grad_ref[k])
        moment_sum = MOMENTUM * wide(moment_ref[k]) + widened
        new_moment_ref[k] = low(moment_sum)
        advance = low(widened + MOMENTUM * moment_sum)
        advance_ref[k] = advance
        for which in range(2):
            copies.append(outgoing(k, which))
            copies[-1].start()
        upper = lax.dot_general(
            advance[:, :middle], advance, contract, preferred_element_type=jnp.float32
        )
        lower = lax.dot_general(
            advance[:, middle:], advance[:, middle:], contract, preferred_element_type=jnp.float32
        )
        blocks = {}
        for i in range(2):
            for j in range(i, 4):
                blocks[i, j] = upper[i * SIDE : (i + 1) * SIDE, j * SIDE : (j + 1) * SIDE]
            for j in range(i, 2):
                blocks[i + 2, j + 2] = lower[i * SIDE : (i + 1) * SIDE, j * SIDE : (j + 1) * SIDE]
        packed = pack(blocks, GRAM_ROWS)
        distance, mine = carried(k)
        mine = mine or k == 0
        natural = core == (0 if mine else 1)
        packed_ref[k, :GRAM_HALF] = jnp.where(natural, packed[:GRAM_HALF], packed[GRAM_HALF:])
        packed_ref[k, GRAM_HALF:] = jnp.where(natural, packed[GRAM_HALF:], packed[:GRAM_HALF])
        if k == 0:
            moves = [
                (packed_ref.at[k, :GRAM_HALF], ours_hbm.at[pl.ds(0, GRAM_HALF)]),
                (packed_ref.at[k, GRAM_HALF:], theirs_hbm.at[pl.ds(0, GRAM_HALF)]),
            ]
        else:
            target = ours_hbm if mine else theirs_hbm
            start = GRAM_HALF + (3 - distance) * GRAM_ROWS
            moves = [(packed_ref.at[k], target.at[pl.ds(start, GRAM_ROWS)])]
        for i, (source, target) in enumerate(moves):
            copies.append(pltpu.make_async_copy(source, target, out_sems.at[2 + i, k]))
            copies[-1].start()
    for copy in copies:
        copy.wait()


def grams(gradients, moments):
    matrices, rows, width = gradients.shape
    anywhere = pl.BlockSpec(memory_space=pl.ANY)
    full = jax.ShapeDtypeStruct(gradients.shape, jnp.bfloat16)
    return pl.pallas_call(
        functools.partial(gram_kernel, matrices),
        out_shape=(
            full,
            full,
            jax.ShapeDtypeStruct((GRAM_HALF + 4 * GRAM_ROWS, SIDE), jnp.bfloat16),
            jax.ShapeDtypeStruct((GRAM_HALF + 3 * GRAM_ROWS, SIDE), jnp.bfloat16),
        ),
        in_specs=[anywhere] * 2,
        out_specs=(anywhere,) * 4,
        scratch_shapes=[pltpu.VMEM(gradients.shape, jnp.bfloat16)] * 4
        + [
            pltpu.VMEM((matrices, GRAM_ROWS, SIDE), jnp.bfloat16),
            pltpu.SemaphoreType.DMA((2, matrices)),
            pltpu.SemaphoreType.DMA((4, matrices)),
        ],
        compiler_params=pltpu.CompilerParams(vmem_limit_bytes=50 * MEBI),
        cost_estimate=pl.CostEstimate(
            flops=2 * gradients.size * width, bytes_accessed=10 * gradients.size, transcendentals=0
        ),
    )(gradients, moments)


def polynomial_kernel(
    place_ref, mine_first, mine_second, theirs_first, theirs_second,
    first_ref, second_ref, ratio_ref,
):
    natural = place_ref[1] == 0
    first = wide(mine_first[...]) + wide(theirs_second[...])
    second = wide(mine_second[...]) + wide(theirs_first[...])
    packed = jnp.concatenate(
        [jnp.where(natural, first, second), jnp.where(natural, second, first)], axis=0
    )
    blocks, extra = unpack_blocks(packed, jnp.float32)
    logits = extra[16:32] + extra[32:48] + extra[48:64]
    peaks = jnp.max(logits, axis=0, keepdims=True)
    ratio_ref[...] = jnp.sqrt(jnp.minimum(1.0, CLIP_LIMIT / peaks))
    corners = off_corner(blocks)
    gram = jnp.concatenate(
        [
            jnp.concatenate([corner(blocks, 0), corners], axis=1),
            jnp.concatenate([corners.T, corner(blocks, 2)], axis=1),
        ],
        axis=0,
    )
    width = gram.shape[0]
    rows = lax.broadcasted_iota(jnp.int32, (width, width), 0)
    columns = lax.broadcasted_iota(jnp.int32, (width, width), 1)
    diagonal = rows == columns
    norm = jnp.sqrt(jnp.sum(jnp.where(diagonal, gram, 0.0)))
    scale = 1.0 / (norm + EPSILON)
    gram = gram * scale * scale

    def poly(gram):
        return SECOND_COEFF * gram + THIRD_COEFF * product(gram, gram)

    def following(gram, step):
        inner = FIRST_COEFF * gram + product(gram, step)
        return FIRST_COEFF * inner + product(inner, step)

    rest = poly(gram)
    factor = FIRST_COEFF
    gram = following(gram, rest)
    for last in (False, True):
        step = poly(gram)
        if not last:
            gram = following(gram, step)
        rest = FIRST_COEFF * rest + factor * step + product(rest, step)
        factor = factor * FIRST_COEFF
    total = jnp.where(diagonal, rest + factor, rest) * scale
    packed = pack(cut_blocks(total), PACKED, residuals=True)
    first_ref[...] = jnp.where(natural, packed[:HALF], packed[HALF:])
    second_ref[...] = jnp.where(natural, packed[HALF:], packed[:HALF])


def polynomial(place, mine, theirs):
    width = 4 * SIDE
    whole = pl.BlockSpec(memory_space=pltpu.VMEM)
    half = jax.ShapeDtypeStruct((HALF, SIDE), jnp.bfloat16)
    return pl.pallas_call(
        polynomial_kernel,
        out_shape=(half, half, jax.ShapeDtypeStruct((1, SIDE), jnp.float32)),
        in_specs=[pl.BlockSpec(memory_space=pltpu.SMEM)] + [whole] * 4,
        out_specs=(whole, whole, whole),
        compiler_params=pltpu.CompilerParams(vmem_limit_bytes=40 * MEBI),
        cost_estimate=pl.CostEstimate(
            flops=9 * 2 * width**3, bytes_accessed=6 * PACKED * SIDE, transcendentals=0
        ),
    )(place, *mine, *theirs)


def finish(place, ratios, advance, weights, parts, results):
    matrices, rows, width = advance.shape
    pieces = []
    for halves, _, _ in parts:
        for array, _ in halves:
            if not any(array is piece for piece in pieces):
                pieces.append(array)
    places = [
        [([array is piece for piece in pieces].index(True), row) for array, row in halves]
        for halves, _, _ in parts
    ]
    count = len(parts)
    middle = width // 2
    scaling = 0.2 * math.sqrt(max(rows * matrices * 2, width))

    def index(step, place):
        chosen = 0
        for k, (_, distance, along) in enumerate(parts):
            below = place[1] == (0 if along else 1)
            signed = jnp.where(below, matrices - distance, distance)
            chosen = jnp.where(step == k, signed, chosen)
        return lax.rem(place[0] + chosen, matrices)

    def kernel(place_ref, ratio_ref, advance_ref, weight_ref, *refs):
        new_weight_ref, update_ref, after_ref = refs[-4:-1]
        after_ref[...] = jnp.zeros_like(after_ref)
        matrix_ref = refs[-1]
        step = pl.program_id(0)

        for k in range(count):

            @pl.when(step == k)
            def _():
                first, second = [refs[i][row : row + HALF] for i, row in places[k]]
                natural = place_ref[1] == (0 if parts[k][2] else 1)
                packed = jnp.concatenate(
                    [jnp.where(natural, first, second), jnp.where(natural, second, first)], axis=0
                )
                blocks, extra = unpack_blocks(packed, jnp.bfloat16)
                matrix_ref[:middle, :middle] = corner(blocks, 0)
                matrix_ref[:middle, middle:] = off_corner(blocks)
                matrix_ref[middle:width, middle:] = corner(blocks, 2)
                for i in range(4):
                    matrix_ref[width:, i * SIDE : (i + 1) * SIDE] = low(
                        jnp.broadcast_to(extra[4 + i : 5 + i], (16, SIDE))
                    )

        which = index(step, place_ref)
        lane = lax.broadcasted_iota(jnp.int32, (1, SIDE), 1)
        head = (which // 2) * (SIDE * 2 // matrices) + (place_ref[0] * 2 + place_ref[1]) * 2
        row = lax.broadcasted_iota(jnp.int32, (rows, 1), 0)
        factor = jnp.zeros((rows, 1), jnp.float32)
        for k in range(rows // DK):
            ratio = jnp.sum(
                jnp.where(lane == head + k, ratio_ref[...], 0.0), axis=1, keepdims=True
            )
            factor = jnp.where(row // DK == k, ratio, factor)
        factor = jnp.where(which % 2 == 0, factor, 1.0)
        off = matrix_ref[:middle, middle:]
        left, right = advance_ref[which, :, :middle], advance_ref[which, :, middle:]
        halves = (
            jnp.dot(left, matrix_ref[:middle, :middle], preferred_element_type=jnp.float32)
            + lax.dot_general(
                right, off, (((1,), (1,)), ((), ())), preferred_element_type=jnp.float32
            ),
            jnp.dot(left, off, preferred_element_type=jnp.float32)
            + jnp.dot(right, matrix_ref[middle:width, middle:], preferred_element_type=jnp.float32),
        )
        for k, values in enumerate((left, right)):
            columns = slice(k * middle, (k + 1) * middle)
            rest = wide(matrix_ref[width : width + 1, columns])
            scaled = scaling * (halves[k] + wide(values) * rest)
            update_ref[0, :, columns] = low(scaled)
            new_weight = (wide(weight_ref[which, :, columns]) * SHRINK - LEARN_RATE * scaled) * factor
            new_weight_ref[0, :, columns] = low(new_weight)

    full = pl.BlockSpec((1, rows, width), lambda step, place: (index(step, place), 0, 0))
    held = pl.BlockSpec(memory_space=pltpu.VMEM)
    one_row = pl.BlockSpec((1, SIDE), lambda step, place: (0, 0))
    anywhere = pl.BlockSpec(memory_space=pl.ANY)
    shape = jax.ShapeDtypeStruct(advance.shape, jnp.bfloat16)
    carry = [] if results is None else list(results)
    first_carried = 4 + len(pieces)
    return pl.pallas_call(
        kernel,
        out_shape=(
            shape,
            shape,
            jax.ShapeDtypeStruct((1, SIDE), jnp.bfloat16),
        ),
        grid_spec=pltpu.PrefetchScalarGridSpec(
            num_scalar_prefetch=1,
            grid=(count,),
            in_specs=[one_row, held, held]
            + [pl.BlockSpec(half.shape, lambda step, place: (0, 0)) for half in pieces]
             + [anywhere] * len(carry),
            out_specs=(full, full, one_row),
            scratch_shapes=[pltpu.VMEM((width + 16, width), jnp.bfloat16)],
        ),
        input_output_aliases={first_carried + k: k for k in range(len(carry))},
        compiler_params=pltpu.CompilerParams(vmem_limit_bytes=48 * MEBI),
        cost_estimate=pl.CostEstimate(
            flops=2 * count * rows * width * width,
            bytes_accessed=count * (8 * rows * width + 2 * PACKED * SIDE),
            transcendentals=0,
        ),
    )(
        place,
        ratios,
        advance,
        weights,
        *pieces,
        *carry,
    )


def observed(head_logits, layers):
    parties, observers = lax.axis_size("dp"), lax.axis_size("mp")
    hops = (0, 1, 2, 1)
    flips = sorted(range(observers), key=lambda flip: -hops[flip // 4] - hops[flip % 4])
    dp = lax.axis_index("dp")
    flip = sum(jnp.where(dp == k, flips[k], 0) for k in range(parties))
    start = jnp.bitwise_xor(lax.axis_index("mp"), flip) * layers
    pairs = [
        (k * observers + i, k * observers + (i ^ flips[k]))
        for k in range(parties)
        for i in range(observers)
    ]
    sent = lax.dynamic_slice_in_dim(head_logits[0], start, layers, 0)
    return lax.ppermute(sent, ("dp", "mp"), pairs).reshape(1, -1)


def gram_rows(values):
    parties = lax.axis_size("dp")
    dp = lax.axis_index("dp")
    high = lax.reduce_precision(values, 8, 7)
    middle = lax.reduce_precision(values - high, 8, 7)
    rest = values - high - middle
    row = lax.broadcasted_iota(jnp.int32, (GRAM_ROWS - SQUARES, 1), 0)
    kind, slot = row // parties, row % parties
    chosen = jnp.where(kind == 1, high, jnp.where(kind == 2, middle, rest))
    return low(jnp.where(jnp.logical_and(kind > 0, slot == dp), chosen, 0.0))


def shards(gradients, moments, weights, head_logits):
    layers, kind_count, row_count, latent_width = gradients.shape
    matrices = layers * kind_count
    parties = lax.axis_size("dp")
    dp = lax.axis_index("dp")
    core = dp % 2
    place = jnp.stack([dp // 2, core]).astype(jnp.int32)
    stacked = (matrices, row_count, latent_width)

    swap_pairs = [(i, i ^ 1) for i in range(parties)]

    def swap(value):
        return lax.ppermute(value, "dp", swap_pairs)

    def onward(value, distance):
        pairs = [(i, (i + 2 * distance * (1 - 2 * (i % 2))) % parties) for i in range(parties)]
        return lax.ppermute(value, "dp", pairs)

    values = observed(head_logits, layers)
    new_moments, advance, ours, theirs = grams(
        gradients.reshape(stacked), moments.reshape(stacked)
    )
    values, theirs = lax.optimization_barrier((values, theirs))
    rows = gram_rows(values)
    both_rows = rows + swap(rows)
    arrived = swap(theirs)

    def in_first(rows):
        rows = jnp.where(core == 0, 0.0, wide(rows))
        return jnp.pad(rows, ((SQUARES - GRAM_HALF, 0), (0, 0)))

    def in_second(rows):
        rows = jnp.where(core == 0, wide(rows), 0.0)
        return jnp.pad(rows, ((SQUARES - GRAM_HALF, 0), (0, 0)))

    def half(k):
        part = slice(k * GRAM_HALF, (k + 1) * GRAM_HALF)
        end = in_first(both_rows) if k == 0 or k % 2 else in_second(both_rows)
        return wide(ours[part]) + wide(arrived[part]) + end

    halves = [low(half(k)) for k in range(3)] + [half(k) for k in range(3, 7)]
    own = [wide(ours[k * GRAM_HALF : (k + 1) * GRAM_HALF]) for k in (7, 8)]
    halves = lax.optimization_barrier(halves)

    def hop(value):
        return wide(onward(low(value), 1))

    far = wide(onward(halves[0], 2))
    first, second = wide(onward(halves[1], 1)), wide(onward(halves[2], 1))
    first, second = hop(halves[3] + first + far), hop(halves[4] + second)
    first, second = hop(halves[5] + first), hop(halves[6] + second)
    second = low(second + own[1] + in_second(rows))
    first = low(first + own[0] + in_first(rows))
    first, second, ratios = polynomial(place, (first, second), (swap(first), swap(second)))

    def final(parts, results):
        *results, after = finish(
            place, ratios, advance, weights.reshape(stacked), parts, results
        )
        return results, after

    pieces = [(first, second)]
    for distance in (1, 2, 3):
        first, second = onward(first, 1), onward(second, 1)
        if distance == 2:
            far = onward(first, 2)
        pieces.append((first, second))
    along = [([(half, 0) for half in pieces[k]], k, True) for k in range(4)]
    results, _ = final(along[:1], None)
    results, after = final(along[1:2], results)
    near = [half for halves in pieces[1:3] for half in halves]
    other_near = swap(jnp.concatenate(near, axis=0) + after)
    results, after = final(
        [
            ([(other_near, 0), (other_near, HALF)], 1, False),
            along[2],
            ([(other_near, 2 * HALF), (other_near, 3 * HALF)], 2, False),
        ],
        results,
    )
    other_remote = swap(jnp.concatenate([*pieces[3], far], axis=0) + after)
    results, _ = final(along[3:], results)
    (new_weights, updates), _ = final(
        [
            ([(other_remote, 0), (other_remote, HALF)], 3, False),
            ([(far, 0), (other_remote, 2 * HALF)], 4, True),
        ],
        results,
    )
    whole = weights.shape
    return (new_weights.reshape(whole), new_moments.reshape(whole), updates.reshape(whole))


def solution(mesh):
    return jax.shard_map(
        shards,
        mesh=mesh,
        in_specs=(
            P("mp", None, "dp", None),
            P("mp", None, "dp", None),
            P("mp", None, "dp", None),
            P("mp", None, None),
        ),
        out_specs=(P("mp", None, "dp", None), P("mp", None, "dp", None), P("mp", None, "dp", None)),
        check_vma=False,
    )
```

```python
import math

import jax
import jax.numpy as jnp
from jax import lax
from jax.experimental import pallas as pl
from jax.experimental.pallas import tpu as pltpu
from jax.sharding import PartitionSpec as P

DK = 128
SIDE = 128
SQUARES = 8 * SIDE
GRAM_ROWS = SQUARES + 64
GRAM_HALF = GRAM_ROWS // 2
PACKED = SQUARES + 32
HALF = PACKED // 2
MEBI = 1024 * 1024

FIRST_COEFF = 3.4445
SECOND_COEFF = -4.775
THIRD_COEFF = 2.0315
MOMENTUM = 0.95
LEARN_RATE = 0.1
SHRINK = 0.99
CLIP_LIMIT = 100.0
EPSILON = 1e-07


def low(value):
    return value.astype(jnp.bfloat16)


def wide(value):
    return value.astype(jnp.float32)


def product(left, right):
    return jnp.dot(low(left), low(right), preferred_element_type=jnp.float32)


def square_iota(dimension):
    return lax.broadcasted_iota(jnp.int32, (SIDE, SIDE), dimension)


def diagonal_row(block):
    return jnp.sum(jnp.where(square_iota(0) == square_iota(1), block, 0.0), axis=0, keepdims=True)


ORDER = ((0, 1), (0, 2), (0, 3)), ((1, 2), (1, 3), (2, 3))


def pack(blocks, rows, residuals=False, peaks=None):
    upper = square_iota(0) <= square_iota(1)
    pieces = []
    for which in range(2):
        even, odd = blocks[2 * which, 2 * which], blocks[2 * which + 1, 2 * which + 1]
        pieces.append(jnp.where(upper, even, odd))
        pieces += [blocks[name] for name in ORDER[which]]
    row = lax.broadcasted_iota(jnp.int32, (rows - SQUARES, SIDE), 0)
    extra = jnp.zeros(row.shape, jnp.float32)
    for i in range(4):
        values = diagonal_row(blocks[i, i])
        extra = jnp.where(row == i, values, extra)
        if residuals:
            extra = jnp.where(row == 4 + i, values - wide(low(values)), extra)
    if peaks is not None:
        for i in range(3):
            extra = jnp.where(row == 8 + i, peaks, extra)
            peaks = peaks - wide(low(peaks))
    return jnp.concatenate([low(piece) for piece in pieces + [extra]], axis=0)


def unpack_blocks(packed, dtype):
    rows, columns = square_iota(0), square_iota(1)
    extra = wide(packed[SQUARES:])
    blocks = {}
    for which in range(2):
        pieces = [packed[(4 * which + k) * SIDE : (4 * which + k + 1) * SIDE] for k in range(4)]
        both = wide(pieces[0])
        turned = both.T
        first, second = extra[2 * which : 2 * which + 1], extra[2 * which + 1 : 2 * which + 2]
        even = jnp.where(rows < columns, both, jnp.where(rows > columns, turned, first))
        odd = jnp.where(rows > columns, both, jnp.where(rows < columns, turned, second))
        blocks[2 * which, 2 * which] = even.astype(dtype)
        blocks[2 * which + 1, 2 * which + 1] = odd.astype(dtype)
        for name, piece in zip(ORDER[which], pieces[1:]):
            blocks[name] = piece.astype(dtype)
    return blocks, extra


def corner(blocks, i):
    right = blocks[i, i + 1]
    return jnp.concatenate(
        [
            jnp.concatenate([blocks[i, i], right], axis=1),
            jnp.concatenate([wide(right).T.astype(right.dtype), blocks[i + 1, i + 1]], axis=1),
        ],
        axis=0,
    )


def off_corner(blocks):
    return jnp.concatenate(
        [jnp.concatenate([blocks[i, 2], blocks[i, 3]], axis=1) for i in (0, 1)], axis=0
    )


def cut_blocks(matrix):
    return {
        (i, j): matrix[i * SIDE : (i + 1) * SIDE, j * SIDE : (j + 1) * SIDE]
        for i in range(4)
        for j in range(i, 4)
    }


def carried(step):
    return 4 - (step + 1) // 2, (step % 2) == 1


def gram_kernel(
    grad_hbm, moment_hbm,
    new_moment_hbm, advance_hbm, mine_hbm, theirs_hbm, far_mine_hbm, their_first_hbm, own_hbm,
    grad_ref, moment_ref, new_moment_ref, advance_ref, packed_ref, in_sems, out_sems,
):
    matrices, rows, width = grad_ref.shape
    dp = lax.axis_index("dp")
    chip, core = dp // 2, dp % 2
    middle = width // 2
    contract = (((0,), (0,)), ((), ()))

    def place_of(step):
        distance, mine = carried(step)
        up = core == (0 if mine else 1)
        return lax.rem(chip + jnp.where(up, distance, matrices - distance), matrices)

    def incoming(step, which):
        source, target = ((grad_hbm, grad_ref), (moment_hbm, moment_ref))[which]
        return pltpu.make_async_copy(
            source.at[place_of(step)], target.at[step], in_sems.at[which, step]
        )

    def outgoing(step, which):
        source, target = ((new_moment_ref, new_moment_hbm), (advance_ref, advance_hbm))[which]
        return pltpu.make_async_copy(
            source.at[step], target.at[place_of(step)], out_sems.at[which, step]
        )

    def packed_copy(source, target, sem):
        return pltpu.make_async_copy(source, target, sem)

    for step in range(matrices):
        incoming(step, 0).start()
        incoming(step, 1).start()
    copies = []
    for step in range(matrices):
        incoming(step, 0).wait()
        incoming(step, 1).wait()
        widened = wide(grad_ref[step])
        moment_sum = MOMENTUM * wide(moment_ref[step]) + widened
        new_moment_ref[step] = low(moment_sum)
        advance = low(widened + MOMENTUM * moment_sum)
        advance_ref[step] = advance
        for which in range(2):
            copies.append(outgoing(step, which))
            copies[-1].start()
        upper = lax.dot_general(
            advance[:, :middle], advance, contract, preferred_element_type=jnp.float32
        )
        lower = lax.dot_general(
            advance[:, middle:], advance[:, middle:], contract, preferred_element_type=jnp.float32
        )
        blocks = {}
        for i in range(2):
            for j in range(i, 4):
                blocks[i, j] = upper[i * SIDE : (i + 1) * SIDE, j * SIDE : (j + 1) * SIDE]
            for j in range(i, 2):
                blocks[i + 2, j + 2] = lower[i * SIDE : (i + 1) * SIDE, j * SIDE : (j + 1) * SIDE]
        packed = pack(blocks, GRAM_ROWS)
        mine = step in (0, matrices - 1) or carried(step)[1]
        natural = core == (0 if mine else 1)
        packed_ref[step, :GRAM_HALF] = jnp.where(natural, packed[:GRAM_HALF], packed[GRAM_HALF:])
        packed_ref[step, GRAM_HALF:] = jnp.where(natural, packed[GRAM_HALF:], packed[:GRAM_HALF])
        if step == 0:
            first, second = packed_ref.at[0, :GRAM_HALF], packed_ref.at[0, GRAM_HALF:]
            copies.append(packed_copy(first, far_mine_hbm, out_sems.at[2, 0]))
            copies[-1].start()
            their_far = their_first_hbm.at[pl.ds(0, GRAM_HALF)]
            copies.append(packed_copy(second, their_far, out_sems.at[3, 0]))
            copies[-1].start()
            continue
        if step == matrices - 1:
            target = own_hbm
        elif mine:
            target = mine_hbm.at[(step - 1) // 2]
        elif step == 2:
            target = their_first_hbm.at[pl.ds(GRAM_HALF, GRAM_ROWS)]
        else:
            target = theirs_hbm.at[(step - 1) // 2 - 1]
        copies.append(packed_copy(packed_ref.at[step], target, out_sems.at[2, step]))
        copies[-1].start()
    for copy in copies:
        copy.wait()


def grams(gradients, moments):
    matrices, rows, width = gradients.shape
    there = pl.BlockSpec(memory_space=pltpu.HBM)
    anywhere = pl.BlockSpec(memory_space=pl.ANY)

    def shape(*sizes):
        return jax.ShapeDtypeStruct(sizes, jnp.bfloat16)

    full = shape(*gradients.shape)
    return pl.pallas_call(
        gram_kernel,
        out_shape=(
            full, full, shape(3, GRAM_ROWS, SIDE), shape(2, GRAM_ROWS, SIDE),
            shape(GRAM_HALF, SIDE), shape(GRAM_HALF + GRAM_ROWS, SIDE), shape(GRAM_ROWS, SIDE),
        ),
        in_specs=[there, there],
        out_specs=(there, there) + (anywhere,) * 5,
        scratch_shapes=[pltpu.VMEM(gradients.shape, jnp.bfloat16)] * 4
        + [
            pltpu.VMEM((matrices, GRAM_ROWS, SIDE), jnp.bfloat16),
            pltpu.SemaphoreType.DMA((2, matrices)),
            pltpu.SemaphoreType.DMA((4, matrices)),
        ],
        compiler_params=pltpu.CompilerParams(vmem_limit_bytes=50 * MEBI),
        cost_estimate=pl.CostEstimate(
            flops=2 * gradients.size * width, bytes_accessed=10 * gradients.size, transcendentals=0
        ),
    )(gradients, moments)


def polynomial_kernel(
    place_ref, mine_first, mine_second, theirs_first, theirs_second, first_ref, second_ref
):
    natural = place_ref[1] == 0
    first = wide(mine_first[...]) + wide(theirs_second[...])
    second = wide(mine_second[...]) + wide(theirs_first[...])
    packed = jnp.concatenate(
        [jnp.where(natural, first, second), jnp.where(natural, second, first)], axis=0
    )
    blocks, extra = unpack_blocks(packed, jnp.float32)
    logits = extra[16:32] + extra[32:48] + extra[48:64]
    peaks = jnp.max(logits, axis=0, keepdims=True)
    corners = off_corner(blocks)
    gram = jnp.concatenate(
        [
            jnp.concatenate([corner(blocks, 0), corners], axis=1),
            jnp.concatenate([corners.T, corner(blocks, 2)], axis=1),
        ],
        axis=0,
    )
    width = gram.shape[0]
    rows = lax.broadcasted_iota(jnp.int32, (width, width), 0)
    columns = lax.broadcasted_iota(jnp.int32, (width, width), 1)
    diagonal = rows == columns
    norm = jnp.sqrt(jnp.sum(jnp.where(diagonal, gram, 0.0)))
    scale = 1.0 / (norm + EPSILON)
    gram = gram * scale * scale

    def poly(gram):
        return SECOND_COEFF * gram + THIRD_COEFF * product(gram, gram)

    def following(gram, step):
        inner = FIRST_COEFF * gram + product(gram, step)
        return FIRST_COEFF * inner + product(inner, step)

    rest = poly(gram)
    factor = FIRST_COEFF
    gram = following(gram, rest)
    for last in (False, True):
        step = poly(gram)
        if not last:
            gram = following(gram, step)
        rest = FIRST_COEFF * rest + factor * step + product(rest, step)
        factor = factor * FIRST_COEFF
    total = jnp.where(diagonal, rest + factor, rest) * scale
    packed = pack(cut_blocks(total), PACKED, residuals=True, peaks=peaks)
    first_ref[...] = jnp.where(natural, packed[:HALF], packed[HALF:])
    second_ref[...] = jnp.where(natural, packed[HALF:], packed[:HALF])


def polynomial(place, mine, theirs):
    width = 4 * SIDE
    whole = pl.BlockSpec(memory_space=pltpu.VMEM)
    half = jax.ShapeDtypeStruct((HALF, SIDE), jnp.bfloat16)
    return pl.pallas_call(
        polynomial_kernel,
        out_shape=(half, half),
        in_specs=[pl.BlockSpec(memory_space=pltpu.SMEM)] + [whole] * 4,
        out_specs=(whole, whole),
        compiler_params=pltpu.CompilerParams(vmem_limit_bytes=40 * MEBI),
        cost_estimate=pl.CostEstimate(
            flops=9 * 2 * width**3, bytes_accessed=6 * PACKED * SIDE, transcendentals=0
        ),
    )(place, *mine, *theirs)


def finish(place, peaks, advance, weights, parts, results):
    matrices, rows, width = advance.shape
    pieces = []
    for halves, _, _ in parts:
        for array, _ in halves:
            if not any(array is piece for piece in pieces):
                pieces.append(array)
    places = [
        [([array is piece for piece in pieces].index(True), row) for array, row in halves]
        for halves, _, _ in parts
    ]
    count = len(parts)
    middle = width // 2
    scaling = 0.2 * math.sqrt(max(rows * matrices * 2, width))

    def index(step, place):
        chosen = 0
        for k, (_, distance, along) in enumerate(parts):
            below = place[1] == (0 if along else 1)
            signed = jnp.where(below, matrices - distance, distance)
            chosen = jnp.where(step == k, signed, chosen)
        return lax.rem(place[0] + chosen, matrices)

    def kernel(place_ref, peaks_ref, advance_ref, weight_ref, *refs):
        new_weight_ref, update_ref, peaks_out_ref, after_ref = refs[-5:-1]
        matrix_ref = refs[-1]
        step = pl.program_id(0)

        @pl.when(step == 0)
        def _():
            after_ref[...] = jnp.zeros_like(after_ref)
            known = peaks_ref[...]
            if peaks is None:
                for k in range(count):
                    ends = [wide(refs[i][row + HALF - 32 : row + HALF]) for i, row in places[k]]
                    natural = place_ref[1] == (0 if parts[k][2] else 1)
                    end = jnp.where(natural, ends[1], ends[0])
                    known = jnp.maximum(known, end[8:9] + end[9:10] + end[10:11])
            peaks_out_ref[...] = known

        for k in range(count):

            @pl.when(step == k)
            def _():
                first, second = [refs[i][row : row + HALF] for i, row in places[k]]
                natural = place_ref[1] == (0 if parts[k][2] else 1)
                packed = jnp.concatenate(
                    [jnp.where(natural, first, second), jnp.where(natural, second, first)], axis=0
                )
                blocks, extra = unpack_blocks(packed, jnp.bfloat16)
                matrix_ref[:middle, :middle] = corner(blocks, 0)
                matrix_ref[:middle, middle:] = off_corner(blocks)
                matrix_ref[middle:width, middle:] = corner(blocks, 2)
                for i in range(4):
                    matrix_ref[width:, i * SIDE : (i + 1) * SIDE] = low(
                        jnp.broadcast_to(extra[4 + i : 5 + i], (16, SIDE))
                    )

        which = index(step, place_ref)
        ratios = jnp.sqrt(jnp.minimum(1.0, CLIP_LIMIT / peaks_out_ref[...]))
        lane = lax.broadcasted_iota(jnp.int32, (1, SIDE), 1)
        head = (which // 2) * (SIDE * 2 // matrices) + (place_ref[0] * 2 + place_ref[1]) * 2
        row = lax.broadcasted_iota(jnp.int32, (rows, 1), 0)
        factor = jnp.zeros((rows, 1), jnp.float32)
        for k in range(rows // DK):
            ratio = jnp.sum(
                jnp.where(lane == head + k, ratios, 0.0), axis=1, keepdims=True
            )
            factor = jnp.where(row // DK == k, ratio, factor)
        factor = jnp.where(which % 2 == 0, factor, 1.0)
        off = matrix_ref[:middle, middle:]
        left, right = advance_ref[which, :, :middle], advance_ref[which, :, middle:]
        halves = (
            jnp.dot(left, matrix_ref[:middle, :middle], preferred_element_type=jnp.float32)
            + lax.dot_general(
                right, off, (((1,), (1,)), ((), ())), preferred_element_type=jnp.float32
            ),
            jnp.dot(left, off, preferred_element_type=jnp.float32)
            + jnp.dot(right, matrix_ref[middle:width, middle:], preferred_element_type=jnp.float32),
        )
        for k, values in enumerate((left, right)):
            columns = slice(k * middle, (k + 1) * middle)
            rest = wide(matrix_ref[width : width + 1, columns])
            scaled = scaling * (halves[k] + wide(values) * rest)
            update_ref[0, :, columns] = low(scaled)
            new_weight = (wide(weight_ref[which, :, columns]) * SHRINK - LEARN_RATE * scaled) * factor
            new_weight_ref[0, :, columns] = low(new_weight)

    full = pl.BlockSpec((1, rows, width), lambda step, place: (index(step, place), 0, 0))
    held = pl.BlockSpec(memory_space=pltpu.VMEM)
    one_row = pl.BlockSpec((1, SIDE), lambda step, place: (0, 0))
    anywhere = pl.BlockSpec(memory_space=pl.ANY)
    shape = jax.ShapeDtypeStruct(advance.shape, jnp.bfloat16)
    carry = [] if results is None else list(results)
    first_carried = 4 + len(pieces)
    return pl.pallas_call(
        kernel,
        out_shape=(
            shape,
            shape,
            jax.ShapeDtypeStruct((1, SIDE), jnp.float32),
            jax.ShapeDtypeStruct((1, SIDE), jnp.bfloat16),
        ),
        grid_spec=pltpu.PrefetchScalarGridSpec(
            num_scalar_prefetch=1,
            grid=(count,),
            in_specs=[one_row, held, held]
            + [pl.BlockSpec(half.shape, lambda step, place: (0, 0)) for half in pieces]
             + [anywhere] * len(carry),
            out_specs=(full, full, one_row, one_row),
            scratch_shapes=[pltpu.VMEM((width + 16, width), jnp.bfloat16)],
        ),
        input_output_aliases={first_carried + k: k for k in range(len(carry))},
        compiler_params=pltpu.CompilerParams(vmem_limit_bytes=48 * MEBI),
        cost_estimate=pl.CostEstimate(
            flops=2 * count * rows * width * width,
            bytes_accessed=count * (8 * rows * width + 2 * PACKED * SIDE),
            transcendentals=0,
        ),
    )(
        place,
        jnp.zeros((1, SIDE), jnp.float32) if peaks is None else peaks,
        advance,
        weights,
        *pieces,
        *carry,
    )


def observed(head_logits, layers):
    parties, observers = lax.axis_size("dp"), lax.axis_size("mp")
    dp = lax.axis_index("dp")
    start = jnp.bitwise_xor(lax.axis_index("mp"), dp) * layers
    pairs = [
        (k * observers + i, k * observers + (i ^ k)) for k in range(parties) for i in range(observers)
    ]
    sent = lax.dynamic_slice_in_dim(head_logits[0], start, layers, 0)
    return lax.ppermute(sent, ("dp", "mp"), pairs).reshape(1, -1)


def gram_rows(values):
    parties = lax.axis_size("dp")
    dp = lax.axis_index("dp")
    high = lax.reduce_precision(values, 8, 7)
    middle = lax.reduce_precision(values - high, 8, 7)
    rest = values - high - middle
    row = lax.broadcasted_iota(jnp.int32, (GRAM_ROWS - SQUARES, 1), 0)
    kind, slot = row // parties, row % parties
    chosen = jnp.where(kind == 1, high, jnp.where(kind == 2, middle, rest))
    return low(jnp.where(jnp.logical_and(kind > 0, slot == dp), chosen, 0.0))


def shards(gradients, moments, weights, head_logits):
    layers, kind_count, row_count, latent_width = gradients.shape
    matrices = layers * kind_count
    parties = lax.axis_size("dp")
    dp = lax.axis_index("dp")
    core = dp % 2
    place = jnp.stack([dp // 2, core]).astype(jnp.int32)
    stacked = (matrices, row_count, latent_width)

    swap_pairs = [(i, i ^ 1) for i in range(parties)]

    def swap(value):
        return lax.ppermute(value, "dp", swap_pairs)

    def onward(value, distance):
        pairs = [(i, (i + 2 * distance * (1 - 2 * (i % 2))) % parties) for i in range(parties)]
        return lax.ppermute(value, "dp", pairs)

    new_moments, advance, mine, theirs, far_mine, their_first, own = grams(
        gradients.reshape(stacked), moments.reshape(stacked)
    )
    arrived_first, arrived = swap(their_first), swap(theirs)

    def first_half(distance):
        return wide(mine[3 - distance, :GRAM_HALF]) + wide(arrived[2 - distance, :GRAM_HALF])

    def second_half(distance):
        return wide(mine[3 - distance, GRAM_HALF:]) + wide(arrived[2 - distance, GRAM_HALF:])

    def in_first(rows):
        rows = jnp.where(core == 0, 0.0, wide(rows))
        return jnp.pad(rows, ((SQUARES - GRAM_HALF, 0), (0, 0)))

    def in_second(rows):
        rows = jnp.where(core == 0, wide(rows), 0.0)
        return jnp.pad(rows, ((SQUARES - GRAM_HALF, 0), (0, 0)))

    def hop(value):
        return wide(onward(low(value), 1))

    far = low(wide(far_mine) + wide(arrived_first[:GRAM_HALF]))
    first = low(wide(mine[0, :GRAM_HALF]) + wide(arrived_first[GRAM_HALF : 2 * GRAM_HALF]))
    second = low(wide(mine[0, GRAM_HALF:]) + wide(arrived_first[2 * GRAM_HALF :]))
    far, first, second, head_logits = lax.optimization_barrier((far, first, second, head_logits))
    firsts, seconds = lax.optimization_barrier(
        ([first_half(2), first_half(1)], [second_half(2), second_half(1)])
    )
    values = observed(head_logits, layers)
    far = wide(onward(far, 2))
    first, second = wide(onward(first, 1)), wide(onward(second, 1))
    values, far, first, second = lax.optimization_barrier((values, far, first, second))
    rows = gram_rows(values)
    first, second = (
        hop(firsts[0] + first + far + in_first(rows)),
        hop(seconds[0] + second + in_second(rows)),
    )
    both_rows = lax.optimization_barrier(rows) + lax.optimization_barrier(swap(rows))
    first, second = (
        hop(firsts[1] + first + in_first(both_rows)),
        hop(seconds[1] + second + in_second(both_rows)),
    )
    second = low(second + wide(own[GRAM_HALF:]) + in_second(rows))
    first = low(first + wide(own[:GRAM_HALF]) + in_first(rows))
    first, second = polynomial(place, (first, second), (swap(first), swap(second)))

    def final(peaks, parts, results):
        *results, peaks, after = finish(
            place, peaks, advance, weights.reshape(stacked), parts, results
        )
        return results, peaks, after

    pieces = [(first, second)]
    for distance in (1, 2, 3):
        first, second = onward(first, 1), onward(second, 1)
        if distance == 2:
            far = onward(first, 2)
        pieces.append((first, second))
    near = [half for halves in pieces[1:3] for half in halves]
    other_near = swap(jnp.concatenate(near, axis=0))
    results, peaks, after = final(
        None,
        [
            ([(half, 0) for half in pieces[0]], 0, True),
            ([(half, 0) for half in pieces[1]], 1, True),
            ([(other_near, 0), (other_near, HALF)], 1, False),
            ([(half, 0) for half in pieces[2]], 2, True),
            ([(other_near, 2 * HALF), (other_near, 3 * HALF)], 2, False),
        ],
        None,
    )
    other_remote = swap(jnp.concatenate([*pieces[3], far], axis=0) + after)
    results, _, _ = final(peaks, [([(half, 0) for half in pieces[3]], 3, True)], results)
    (new_weights, updates), _, _ = final(
        peaks,
        [
            ([(other_remote, 0), (other_remote, HALF)], 3, False),
            ([(far, 0), (other_remote, 2 * HALF)], 4, True),
        ],
        results,
    )
    whole = gradients.shape
    return (new_weights.reshape(whole), new_moments.reshape(whole), updates.reshape(whole))


def solution(mesh):
    return jax.shard_map(
        shards,
        mesh=mesh,
        in_specs=(
            P("mp", None, "dp", None),
            P("mp", None, "dp", None),
            P("mp", None, "dp", None),
            P("mp", None, None),
        ),
        out_specs=(P("mp", None, "dp", None), P("mp", None, "dp", None), P("mp", None, "dp", None)),
        check_vma=False,
    )
```

```python
import math

import jax
import jax.numpy as jnp
from jax import lax
from jax.experimental import pallas as pl
from jax.experimental.pallas import tpu as pltpu
from jax.sharding import PartitionSpec as P

DK = 128
SIDE = 128
SQUARES = 8 * SIDE
GRAM_ROWS = SQUARES + 64
GRAM_HALF = GRAM_ROWS // 2
PACKED = SQUARES + 32
HALF = PACKED // 2
MEBI = 1024 * 1024

FIRST_COEFF = 3.4445
SECOND_COEFF = -4.775
THIRD_COEFF = 2.0315
MOMENTUM = 0.95
LEARN_RATE = 0.1
SHRINK = 0.99
CLIP_LIMIT = 100.0
EPSILON = 1e-07


def low(value):
    return value.astype(jnp.bfloat16)


def wide(value):
    return value.astype(jnp.float32)


def product(left, right):
    return jnp.dot(low(left), low(right), preferred_element_type=jnp.float32)


def square_iota(dimension):
    return lax.broadcasted_iota(jnp.int32, (SIDE, SIDE), dimension)


def diagonal_row(block):
    return jnp.sum(jnp.where(square_iota(0) == square_iota(1), block, 0.0), axis=0, keepdims=True)


ORDER = ((0, 1), (0, 2), (0, 3)), ((1, 2), (1, 3), (2, 3))


def pack(blocks, rows, residuals=False, peaks=None):
    upper = square_iota(0) <= square_iota(1)
    pieces = []
    for which in range(2):
        even, odd = blocks[2 * which, 2 * which], blocks[2 * which + 1, 2 * which + 1]
        pieces.append(jnp.where(upper, even, odd))
        pieces += [blocks[name] for name in ORDER[which]]
    row = lax.broadcasted_iota(jnp.int32, (rows - SQUARES, SIDE), 0)
    extra = jnp.zeros(row.shape, jnp.float32)
    for i in range(4):
        values = diagonal_row(blocks[i, i])
        extra = jnp.where(row == i, values, extra)
        if residuals:
            extra = jnp.where(row == 4 + i, values - wide(low(values)), extra)
    if peaks is not None:
        for i in range(3):
            extra = jnp.where(row == 8 + i, peaks, extra)
            peaks = peaks - wide(low(peaks))
    return jnp.concatenate([low(piece) for piece in pieces + [extra]], axis=0)


def unpack_blocks(packed, dtype):
    rows, columns = square_iota(0), square_iota(1)
    extra = wide(packed[SQUARES:])
    blocks = {}
    for which in range(2):
        pieces = [packed[(4 * which + k) * SIDE : (4 * which + k + 1) * SIDE] for k in range(4)]
        both = wide(pieces[0])
        turned = both.T
        first, second = extra[2 * which : 2 * which + 1], extra[2 * which + 1 : 2 * which + 2]
        even = jnp.where(rows < columns, both, jnp.where(rows > columns, turned, first))
        odd = jnp.where(rows > columns, both, jnp.where(rows < columns, turned, second))
        blocks[2 * which, 2 * which] = even.astype(dtype)
        blocks[2 * which + 1, 2 * which + 1] = odd.astype(dtype)
        for name, piece in zip(ORDER[which], pieces[1:]):
            blocks[name] = piece.astype(dtype)
    return blocks, extra


def corner(blocks, i):
    right = blocks[i, i + 1]
    return jnp.concatenate(
        [
            jnp.concatenate([blocks[i, i], right], axis=1),
            jnp.concatenate([wide(right).T.astype(right.dtype), blocks[i + 1, i + 1]], axis=1),
        ],
        axis=0,
    )


def off_corner(blocks):
    return jnp.concatenate(
        [jnp.concatenate([blocks[i, 2], blocks[i, 3]], axis=1) for i in (0, 1)], axis=0
    )


def cut_blocks(matrix):
    return {
        (i, j): matrix[i * SIDE : (i + 1) * SIDE, j * SIDE : (j + 1) * SIDE]
        for i in range(4)
        for j in range(i, 4)
    }


def carried(step):
    return 4 - (step + 1) // 2, (step % 2) == 1


def gram_kernel(
    grad_hbm, moment_hbm,
    new_moment_hbm, advance_hbm, mine_hbm, theirs_hbm, far_mine_hbm, their_first_hbm, own_hbm,
    grad_ref, moment_ref, new_moment_ref, advance_ref, packed_ref, in_sems, out_sems,
):
    matrices, rows, width = grad_ref.shape
    dp = lax.axis_index("dp")
    chip, core = dp // 2, dp % 2
    middle = width // 2
    contract = (((0,), (0,)), ((), ()))

    def place_of(step):
        distance, mine = carried(step)
        up = core == (0 if mine else 1)
        return lax.rem(chip + jnp.where(up, distance, matrices - distance), matrices)

    def incoming(step, which):
        source, target = ((grad_hbm, grad_ref), (moment_hbm, moment_ref))[which]
        return pltpu.make_async_copy(
            source.at[place_of(step)], target.at[step], in_sems.at[which, step]
        )

    def outgoing(step, which):
        source, target = ((new_moment_ref, new_moment_hbm), (advance_ref, advance_hbm))[which]
        return pltpu.make_async_copy(
            source.at[step], target.at[place_of(step)], out_sems.at[which, step]
        )

    def packed_copy(source, target, sem):
        return pltpu.make_async_copy(source, target, sem)

    for step in range(matrices):
        incoming(step, 0).start()
        incoming(step, 1).start()
    copies = []
    for step in range(matrices):
        incoming(step, 0).wait()
        incoming(step, 1).wait()
        widened = wide(grad_ref[step])
        moment_sum = MOMENTUM * wide(moment_ref[step]) + widened
        new_moment_ref[step] = low(moment_sum)
        advance = low(widened + MOMENTUM * moment_sum)
        advance_ref[step] = advance
        for which in range(2):
            copies.append(outgoing(step, which))
            copies[-1].start()
        upper = lax.dot_general(
            advance[:, :middle], advance, contract, preferred_element_type=jnp.float32
        )
        lower = lax.dot_general(
            advance[:, middle:], advance[:, middle:], contract, preferred_element_type=jnp.float32
        )
        blocks = {}
        for i in range(2):
            for j in range(i, 4):
                blocks[i, j] = upper[i * SIDE : (i + 1) * SIDE, j * SIDE : (j + 1) * SIDE]
            for j in range(i, 2):
                blocks[i + 2, j + 2] = lower[i * SIDE : (i + 1) * SIDE, j * SIDE : (j + 1) * SIDE]
        packed = pack(blocks, GRAM_ROWS)
        mine = step in (0, matrices - 1) or carried(step)[1]
        natural = core == (0 if mine else 1)
        packed_ref[step, :GRAM_HALF] = jnp.where(natural, packed[:GRAM_HALF], packed[GRAM_HALF:])
        packed_ref[step, GRAM_HALF:] = jnp.where(natural, packed[GRAM_HALF:], packed[:GRAM_HALF])
        if step == 0:
            first, second = packed_ref.at[0, :GRAM_HALF], packed_ref.at[0, GRAM_HALF:]
            copies.append(packed_copy(first, far_mine_hbm, out_sems.at[2, 0]))
            copies[-1].start()
            their_far = their_first_hbm.at[pl.ds(0, GRAM_HALF)]
            copies.append(packed_copy(second, their_far, out_sems.at[3, 0]))
            copies[-1].start()
            continue
        if step == matrices - 1:
            target = own_hbm
        elif mine:
            target = mine_hbm.at[(step - 1) // 2]
        elif step == 2:
            target = their_first_hbm.at[pl.ds(GRAM_HALF, GRAM_ROWS)]
        else:
            target = theirs_hbm.at[(step - 1) // 2 - 1]
        copies.append(packed_copy(packed_ref.at[step], target, out_sems.at[2, step]))
        copies[-1].start()
    for copy in copies:
        copy.wait()


def grams(gradients, moments):
    matrices, rows, width = gradients.shape
    there = pl.BlockSpec(memory_space=pltpu.HBM)
    anywhere = pl.BlockSpec(memory_space=pl.ANY)

    def shape(*sizes):
        return jax.ShapeDtypeStruct(sizes, jnp.bfloat16)

    full = shape(*gradients.shape)
    return pl.pallas_call(
        gram_kernel,
        out_shape=(
            full, full, shape(3, GRAM_ROWS, SIDE), shape(2, GRAM_ROWS, SIDE),
            shape(GRAM_HALF, SIDE), shape(GRAM_HALF + GRAM_ROWS, SIDE), shape(GRAM_ROWS, SIDE),
        ),
        in_specs=[there, there],
        out_specs=(there, there) + (anywhere,) * 5,
        scratch_shapes=[pltpu.VMEM(gradients.shape, jnp.bfloat16)] * 4
        + [
            pltpu.VMEM((matrices, GRAM_ROWS, SIDE), jnp.bfloat16),
            pltpu.SemaphoreType.DMA((2, matrices)),
            pltpu.SemaphoreType.DMA((4, matrices)),
        ],
        compiler_params=pltpu.CompilerParams(vmem_limit_bytes=50 * MEBI),
        cost_estimate=pl.CostEstimate(
            flops=2 * gradients.size * width, bytes_accessed=10 * gradients.size, transcendentals=0
        ),
    )(gradients, moments)


def polynomial_kernel(
    place_ref, mine_first, mine_second, theirs_first, theirs_second, first_ref, second_ref
):
    natural = place_ref[1] == 0
    first = wide(mine_first[...]) + wide(theirs_second[...])
    second = wide(mine_second[...]) + wide(theirs_first[...])
    packed = jnp.concatenate(
        [jnp.where(natural, first, second), jnp.where(natural, second, first)], axis=0
    )
    blocks, extra = unpack_blocks(packed, jnp.float32)
    logits = extra[16:32] + extra[32:48] + extra[48:64]
    peaks = jnp.max(logits, axis=0, keepdims=True)
    corners = off_corner(blocks)
    gram = jnp.concatenate(
        [
            jnp.concatenate([corner(blocks, 0), corners], axis=1),
            jnp.concatenate([corners.T, corner(blocks, 2)], axis=1),
        ],
        axis=0,
    )
    width = gram.shape[0]
    rows = lax.broadcasted_iota(jnp.int32, (width, width), 0)
    columns = lax.broadcasted_iota(jnp.int32, (width, width), 1)
    diagonal = rows == columns
    norm = jnp.sqrt(jnp.sum(jnp.where(diagonal, gram, 0.0)))
    scale = 1.0 / (norm + EPSILON)
    gram = gram * scale * scale

    def poly(gram):
        return SECOND_COEFF * gram + THIRD_COEFF * product(gram, gram)

    def following(gram, step):
        inner = FIRST_COEFF * gram + product(gram, step)
        return FIRST_COEFF * inner + product(inner, step)

    rest = poly(gram)
    factor = FIRST_COEFF
    gram = following(gram, rest)
    for last in (False, True):
        step = poly(gram)
        if not last:
            gram = following(gram, step)
        rest = FIRST_COEFF * rest + factor * step + product(rest, step)
        factor = factor * FIRST_COEFF
    total = jnp.where(diagonal, rest + factor, rest) * scale
    packed = pack(cut_blocks(total), PACKED, residuals=True, peaks=peaks)
    first_ref[...] = jnp.where(natural, packed[:HALF], packed[HALF:])
    second_ref[...] = jnp.where(natural, packed[HALF:], packed[:HALF])


def polynomial(place, mine, theirs):
    width = 4 * SIDE
    whole = pl.BlockSpec(memory_space=pltpu.VMEM)
    half = jax.ShapeDtypeStruct((HALF, SIDE), jnp.bfloat16)
    return pl.pallas_call(
        polynomial_kernel,
        out_shape=(half, half),
        in_specs=[pl.BlockSpec(memory_space=pltpu.SMEM)] + [whole] * 4,
        out_specs=(whole, whole),
        compiler_params=pltpu.CompilerParams(vmem_limit_bytes=40 * MEBI),
        cost_estimate=pl.CostEstimate(
            flops=9 * 2 * width**3, bytes_accessed=6 * PACKED * SIDE, transcendentals=0
        ),
    )(place, *mine, *theirs)


def finish(place, peaks, advance, weights, parts, results):
    matrices, rows, width = advance.shape
    pieces = []
    for halves, _, _ in parts:
        for array, _ in halves:
            if not any(array is piece for piece in pieces):
                pieces.append(array)
    places = [
        [([array is piece for piece in pieces].index(True), row) for array, row in halves]
        for halves, _, _ in parts
    ]
    count = len(parts)
    middle = width // 2
    scaling = 0.2 * math.sqrt(max(rows * matrices * 2, width))

    def index(step, place):
        chosen = 0
        for k, (_, distance, along) in enumerate(parts):
            below = place[1] == (0 if along else 1)
            signed = jnp.where(below, matrices - distance, distance)
            chosen = jnp.where(step == k, signed, chosen)
        return lax.rem(place[0] + chosen, matrices)

    def kernel(place_ref, peaks_ref, advance_ref, weight_ref, *refs):
        new_weight_ref, update_ref, peaks_out_ref, after_ref = refs[-5:-1]
        matrix_ref = refs[-1]
        step = pl.program_id(0)

        @pl.when(step == 0)
        def _():
            after_ref[...] = jnp.zeros_like(after_ref)
            known = peaks_ref[...]
            if peaks is None:
                for k in range(count):
                    ends = [wide(refs[i][row + HALF - 32 : row + HALF]) for i, row in places[k]]
                    natural = place_ref[1] == (0 if parts[k][2] else 1)
                    end = jnp.where(natural, ends[1], ends[0])
                    known = jnp.maximum(known, end[8:9] + end[9:10] + end[10:11])
            peaks_out_ref[...] = known

        for k in range(count):

            @pl.when(step == k)
            def _():
                first, second = [refs[i][row : row + HALF] for i, row in places[k]]
                natural = place_ref[1] == (0 if parts[k][2] else 1)
                packed = jnp.concatenate(
                    [jnp.where(natural, first, second), jnp.where(natural, second, first)], axis=0
                )
                blocks, extra = unpack_blocks(packed, jnp.bfloat16)
                matrix_ref[:middle, :middle] = corner(blocks, 0)
                matrix_ref[:middle, middle:] = off_corner(blocks)
                matrix_ref[middle:width, middle:] = corner(blocks, 2)
                for i in range(4):
                    matrix_ref[width:, i * SIDE : (i + 1) * SIDE] = low(
                        jnp.broadcast_to(extra[4 + i : 5 + i], (16, SIDE))
                    )

        which = index(step, place_ref)
        ratios = jnp.sqrt(jnp.minimum(1.0, CLIP_LIMIT / peaks_out_ref[...]))
        lane = lax.broadcasted_iota(jnp.int32, (1, SIDE), 1)
        head = (which // 2) * (SIDE * 2 // matrices) + (place_ref[0] * 2 + place_ref[1]) * 2
        row = lax.broadcasted_iota(jnp.int32, (rows, 1), 0)
        factor = jnp.zeros((rows, 1), jnp.float32)
        for k in range(rows // DK):
            ratio = jnp.sum(
                jnp.where(lane == head + k, ratios, 0.0), axis=1, keepdims=True
            )
            factor = jnp.where(row // DK == k, ratio, factor)
        factor = jnp.where(which % 2 == 0, factor, 1.0)
        off = matrix_ref[:middle, middle:]
        left, right = advance_ref[which, :, :middle], advance_ref[which, :, middle:]
        halves = (
            jnp.dot(left, matrix_ref[:middle, :middle], preferred_element_type=jnp.float32)
            + lax.dot_general(
                right, off, (((1,), (1,)), ((), ())), preferred_element_type=jnp.float32
            ),
            jnp.dot(left, off, preferred_element_type=jnp.float32)
            + jnp.dot(right, matrix_ref[middle:width, middle:], preferred_element_type=jnp.float32),
        )
        for k, values in enumerate((left, right)):
            columns = slice(k * middle, (k + 1) * middle)
            rest = wide(matrix_ref[width : width + 1, columns])
            scaled = scaling * (halves[k] + wide(values) * rest)
            update_ref[0, :, columns] = low(scaled)
            new_weight = (wide(weight_ref[which, :, columns]) * SHRINK - LEARN_RATE * scaled) * factor
            new_weight_ref[0, :, columns] = low(new_weight)

    full = pl.BlockSpec((1, rows, width), lambda step, place: (index(step, place), 0, 0))
    held = pl.BlockSpec(memory_space=pltpu.VMEM)
    one_row = pl.BlockSpec((1, SIDE), lambda step, place: (0, 0))
    anywhere = pl.BlockSpec(memory_space=pl.ANY)
    shape = jax.ShapeDtypeStruct(advance.shape, jnp.bfloat16)
    carry = [] if results is None else list(results)
    first_carried = 4 + len(pieces)
    return pl.pallas_call(
        kernel,
        out_shape=(
            shape,
            shape,
            jax.ShapeDtypeStruct((1, SIDE), jnp.float32),
            jax.ShapeDtypeStruct((1, SIDE), jnp.bfloat16),
        ),
        grid_spec=pltpu.PrefetchScalarGridSpec(
            num_scalar_prefetch=1,
            grid=(count,),
            in_specs=[one_row, held, held]
            + [pl.BlockSpec(half.shape, lambda step, place: (0, 0)) for half in pieces]
             + [anywhere] * len(carry),
            out_specs=(full, full, one_row, one_row),
            scratch_shapes=[pltpu.VMEM((width + 16, width), jnp.bfloat16)],
        ),
        input_output_aliases={first_carried + k: k for k in range(len(carry))},
        compiler_params=pltpu.CompilerParams(vmem_limit_bytes=48 * MEBI),
        cost_estimate=pl.CostEstimate(
            flops=2 * count * rows * width * width,
            bytes_accessed=count * (8 * rows * width + 2 * PACKED * SIDE),
            transcendentals=0,
        ),
    )(
        place,
        jnp.zeros((1, SIDE), jnp.float32) if peaks is None else peaks,
        advance,
        weights,
        *pieces,
        *carry,
    )


def observed(head_logits, layers):
    parties, observers = lax.axis_size("dp"), lax.axis_size("mp")
    dp = lax.axis_index("dp")
    start = jnp.bitwise_xor(lax.axis_index("mp"), dp) * layers
    pairs = [
        (k * observers + i, k * observers + (i ^ k)) for k in range(parties) for i in range(observers)
    ]
    sent = lax.dynamic_slice_in_dim(head_logits[0], start, layers, 0)
    return lax.ppermute(sent, ("dp", "mp"), pairs).reshape(1, -1)


def gram_rows(values):
    parties = lax.axis_size("dp")
    dp = lax.axis_index("dp")
    high = lax.reduce_precision(values, 8, 7)
    middle = lax.reduce_precision(values - high, 8, 7)
    rest = values - high - middle
    row = lax.broadcasted_iota(jnp.int32, (GRAM_ROWS - SQUARES, 1), 0)
    kind, slot = row // parties, row % parties
    chosen = jnp.where(kind == 1, high, jnp.where(kind == 2, middle, rest))
    return low(jnp.where(jnp.logical_and(kind > 0, slot == dp), chosen, 0.0))


def shards(gradients, moments, weights, head_logits):
    layers, kind_count, row_count, latent_width = gradients.shape
    matrices = layers * kind_count
    parties = lax.axis_size("dp")
    dp = lax.axis_index("dp")
    core = dp % 2
    place = jnp.stack([dp // 2, core]).astype(jnp.int32)
    stacked = (matrices, row_count, latent_width)

    swap_pairs = [(i, i ^ 1) for i in range(parties)]

    def swap(value):
        return lax.ppermute(value, "dp", swap_pairs)

    def onward(value, distance):
        pairs = [(i, (i + 2 * distance * (1 - 2 * (i % 2))) % parties) for i in range(parties)]
        return lax.ppermute(value, "dp", pairs)

    new_moments, advance, mine, theirs, far_mine, their_first, own = grams(
        gradients.reshape(stacked), moments.reshape(stacked)
    )
    arrived_first, arrived = swap(their_first), swap(theirs)

    def first_half(distance):
        return wide(mine[3 - distance, :GRAM_HALF]) + wide(arrived[2 - distance, :GRAM_HALF])

    def second_half(distance):
        return wide(mine[3 - distance, GRAM_HALF:]) + wide(arrived[2 - distance, GRAM_HALF:])

    def in_first(rows):
        rows = jnp.where(core == 0, 0.0, wide(rows))
        return jnp.pad(rows, ((SQUARES - GRAM_HALF, 0), (0, 0)))

    def in_second(rows):
        rows = jnp.where(core == 0, wide(rows), 0.0)
        return jnp.pad(rows, ((SQUARES - GRAM_HALF, 0), (0, 0)))

    def hop(value):
        return wide(onward(low(value), 1))

    far = low(wide(far_mine) + wide(arrived_first[:GRAM_HALF]))
    first = low(wide(mine[0, :GRAM_HALF]) + wide(arrived_first[GRAM_HALF : 2 * GRAM_HALF]))
    second = low(wide(mine[0, GRAM_HALF:]) + wide(arrived_first[2 * GRAM_HALF :]))
    far, first, second, head_logits = lax.optimization_barrier((far, first, second, head_logits))
    firsts, seconds = lax.optimization_barrier(
        ([first_half(2), first_half(1)], [second_half(2), second_half(1)])
    )
    values = observed(head_logits, layers)
    far = wide(onward(far, 2))
    first, second = wide(onward(first, 1)), wide(onward(second, 1))
    values, far, first, second = lax.optimization_barrier((values, far, first, second))
    rows = gram_rows(values)
    first, second = (
        hop(firsts[0] + first + far + in_first(rows)),
        hop(seconds[0] + second + in_second(rows)),
    )
    both_rows = lax.optimization_barrier(rows) + lax.optimization_barrier(swap(rows))
    first, second = (
        hop(firsts[1] + first + in_first(both_rows)),
        hop(seconds[1] + second + in_second(both_rows)),
    )
    second = low(second + wide(own[GRAM_HALF:]) + in_second(rows))
    first = low(first + wide(own[:GRAM_HALF]) + in_first(rows))
    first, second = polynomial(place, (first, second), (swap(first), swap(second)))

    def final(peaks, parts, results):
        *results, peaks, after = finish(
            place, peaks, advance, weights.reshape(stacked), parts, results
        )
        return results, peaks, after

    pieces = [(first, second)]
    for distance in (1, 2, 3):
        first, second = onward(first, 1), onward(second, 1)
        if distance == 2:
            far = onward(first, 2)
        pieces.append((first, second))
    near = [half for halves in pieces[1:3] for half in halves]
    other_near = swap(jnp.concatenate(near, axis=0))
    results, peaks, after = final(
        None,
        [
            ([(half, 0) for half in pieces[0]], 0, True),
            ([(half, 0) for half in pieces[1]], 1, True),
            ([(other_near, 0), (other_near, HALF)], 1, False),
            ([(half, 0) for half in pieces[2]], 2, True),
            ([(other_near, 2 * HALF), (other_near, 3 * HALF)], 2, False),
        ],
        None,
    )
    other_remote = swap(jnp.concatenate(pieces[3], axis=0) + after)
    results, _, after = final(peaks, [([(half, 0) for half in pieces[3]], 3, True)], results)
    other_far = swap(far + after)
    (new_weights, updates), _, _ = final(
        peaks,
        [
            ([(other_remote, 0), (other_remote, HALF)], 3, False),
            ([(far, 0), (other_far, 0)], 4, True),
        ],
        results,
    )
    whole = gradients.shape
    return (new_weights.reshape(whole), new_moments.reshape(whole), updates.reshape(whole))


def solution(mesh):
    return jax.shard_map(
        shards,
        mesh=mesh,
        in_specs=(
            P("mp", None, "dp", None),
            P("mp", None, "dp", None),
            P("mp", None, "dp", None),
            P("mp", None, None),
        ),
        out_specs=(P("mp", None, "dp", None), P("mp", None, "dp", None), P("mp", None, "dp", None)),
        check_vma=False,
    )
```
